32 devices in a mesh: grp: 2 (over y), br: 4 (over z), rhs: 2 (over x), sub: 2 (over core).
Axes of the slice: x: 2, y: 2, z: 4, core: 2. Of those that a mesh axis runs over, the one named last changes fastest.
Arguments:
- sources: bfloat16 [64, 64, 2048], P(('grp', 'rhs', 'sub'), 'br'), parts along dimension 0, may hold values from -6 to 6
- leaf_basis: bfloat16 [64, 64, 4096], P(('grp', 'rhs', 'sub'), 'br'), parts along dimension 0, may hold values from -0.75 to 0.75
- transfer: bfloat16 [3, 4, 4096], replicated, may hold values from -0.375 to 0.375
- coupling: bfloat16 [4, 49, 4096], replicated, may hold values from -0.15625 to 0.15625
- near_table: bfloat16 [9, 4096], replicated, may hold values from -0.25 to 0.25
- near_mask: int32 [64, 64, 9], P(('grp', 'rhs', 'sub'), 'br'), parts along dimension 0, may hold values 0 or 1
- mask_leaf: int32 [64, 64, 27], P(('grp', 'rhs', 'sub'), 'br'), parts along dimension 0, may hold values 0 or 1
- mask_mid: int32 [32, 32, 27], P(('grp', 'rhs', 'sub'), 'br'), parts along dimension 0, may hold values 0 or 1
- mask_upper: int32 [16, 16, 27], P('grp', 'br'), parts along dimension 0, may hold values 0 or 1
- mask_top: int32 [8, 8, 27], P('grp', 'br'), parts along dimension 0, may hold values 0 or 1
Outputs:
- result: bfloat16 [64, 64, 2048], P(('grp', 'rhs', 'sub'), 'br'), parts along dimension 0
The draws below stay inside these ranges and needn't reach their ends.
There are 2 independent parts, one for each index of `grp`. The reference program is written for one: setup_inputs(seed, part) draws one part's arguments, and reference() takes and returns one part's arrays. A program takes and returns all parts, laid end to end along the dimension named above; an argument that names none is the same for every part. Nothing has to cross between parts.
Inputs may be any that keep to these rules, and one draw needn't show every extreme that they name: `near_mask`: 1 keeps a neighbour in a leaf's near-field list, 0 marks a padded entry. `mask_leaf`: 1 keeps an entry of a node's coupling list, 0 marks a padded one. `mask_mid`: 1 keeps an entry of a node's coupling list, 0 marks a padded one. `mask_upper`: 1 keeps an entry of a node's coupling list, 0 marks a padded one. `mask_top`: 1 keeps an entry of a node's coupling list, 0 marks a padded one.
All inputs are finite; a program needn't handle non-finite values. No bound on the sum of `near_mask` or of `mask_leaf` or of `mask_mid` or of `mask_upper` or of `mask_top` on one device may be relied on, other than what follows from the above.
Results may differ from the reference program's by a relative error of at most 0.017.
Values may be sent and summed in bfloat16 or wider, within the bound.
No kernel may reach another device: no remote copies, remote signals or barrier semaphores. Data moves between devices by JAX's collectives and lax.ppermute only.
A program may use at most 192 MiB of HBM per device.

```python
import jax
import jax.numpy as jnp
from jax import lax

LEAF = 64
RANK = 64
SIDES = 32
PRODUCTS = 3
ROWS = 32
COLS = 64


def set_ends(result, rng, smallest, largest):
    dims = result.shape
    spot = [jax.random.randint(jax.random.fold_in(rng, axis), (), 0, dims[axis]) for axis in range(len(dims))]
    result = result.at[tuple(spot)].set(smallest)
    longest = dims.index(max(dims))
    spot[longest] = (spot[longest] + 1) % dims[longest]
    return result.at[tuple(spot)].set(largest)


def shard_levels(stream_key, dims, pieces, least, top_value):
    level, own = 1.0, jax.random.fold_in(stream_key, 6)
    for position, blocks in pieces:
        steps = jnp.exp(jax.random.uniform(jax.random.fold_in(own, position), (blocks,), jnp.float32, least / len(pieces), top_value / len(pieces)))
        level = level * jnp.repeat(steps, dims[position] // blocks).reshape([-1 if axis == position else 1 for axis in range(len(dims))])
    return level


def centred(rng, extent, deviation, most, cuts=(), held_as=jnp.bfloat16):
    drawn = jax.random.normal(rng, extent, jnp.float32) * deviation
    if len(cuts) > 0:
        drawn = shard_levels(rng, extent, cuts, -0.22, 0.18) * drawn
    return jnp.clip(drawn, min=-most, max=most).astype(held_as)


def setup_inputs(seed: int = 0, part: int = 0) -> dict:
    arg_keys = jax.random.split(jax.random.key(seed), 11)
    own_keys = jax.random.split(jax.random.fold_in(arg_keys[10], part), 11)
    return {
        "sources": centred(own_keys[0], (ROWS, COLS, SIDES * LEAF), 1.0, 6.0, ((0, 4), (1, 4))),
        "leaf_basis": centred(own_keys[1], (ROWS, COLS, LEAF * RANK), LEAF ** -0.5, 0.75, ((0, 4), (1, 4))),
        "transfer": centred(arg_keys[2], (3, 4, RANK * RANK), (4 * RANK) ** -0.5, 0.375),
        "coupling": centred(arg_keys[3], (4, 49, RANK * RANK), (27 * RANK) ** -0.5, 0.15625),
        "near_table": centred(arg_keys[4], (9, LEAF * LEAF), (9 * LEAF) ** -0.5, 0.25),
        "near_mask": set_ends((jax.random.randint(own_keys[5], (ROWS, COLS, 9), 0, 4) < 3).astype(jnp.int32), jax.random.fold_in(own_keys[5], 1), 0, 1),
        "mask_leaf": set_ends((jax.random.randint(own_keys[6], (ROWS, COLS, 27), 0, 4) < 3).astype(jnp.int32), jax.random.fold_in(own_keys[6], 1), 0, 1),
        "mask_mid": set_ends((jax.random.randint(own_keys[7], (ROWS // 2, COLS // 2, 27), 0, 4) < 3).astype(jnp.int32), jax.random.fold_in(own_keys[7], 1), 0, 1),
        "mask_upper": set_ends((jax.random.randint(own_keys[8], (ROWS // 4, COLS // 4, 27), 0, 4) < 3).astype(jnp.int32), jax.random.fold_in(own_keys[8], 1), 0, 1),
        "mask_top": set_ends((jax.random.randint(own_keys[9], (ROWS // 8, COLS // 8, 27), 0, 4) < 3).astype(jnp.int32), jax.random.fold_in(own_keys[9], 1), 0, 1),
    }


def to_half(value):
    return lax.optimization_barrier(value.astype(jnp.bfloat16))


def couple_whole(coeffs, slot_mask, op_table):
    span_rows, span_cols = coeffs.shape[0], coeffs.shape[1]
    grid_vals = coeffs.astype(jnp.float32).reshape(span_rows, span_cols, SIDES, RANK)
    padded = jnp.pad(grid_vals, ((2, 2), (2, 2), (0, 0), (0, 0)))
    matrices = op_table.astype(jnp.float32).reshape(49, RANK, RANK)
    total = jnp.zeros((span_rows // 2, 2, span_cols // 2, 2, SIDES, RANK), jnp.float32)
    for row_par in range(2):
        for col_par in range(2):
            slot_index = 0
            running = jnp.zeros((span_rows // 2, span_cols // 2, SIDES, RANK), jnp.float32)
            for win_row in range(6):
                for win_col in range(6):
                    row_step = win_row - 2 - row_par
                    col_step = win_col - 2 - col_par
                    if abs(row_step) <= 1 and abs(col_step) <= 1:
                        continue
                    source = padded[win_row:win_row + span_rows:2, win_col:win_col + span_cols:2]
                    kept_mask = slot_mask[row_par::2, col_par::2, slot_index].astype(jnp.float32)
                    running = running + jnp.einsum("ijsr,rt->ijst", source * kept_mask[:, :, None, None], matrices[(row_step + 3) * 7 + col_step + 3])
                    slot_index = slot_index + 1
            total = total.at[:, row_par, :, col_par].set(running)
    return total.reshape(span_rows, span_cols, SIDES * RANK)


def upward(child, transfer_level):
    span_rows, span_cols = child.shape[0] // 2, child.shape[1] // 2
    blocks = child.astype(jnp.float32).reshape(span_rows, 2, span_cols, 2, SIDES, RANK)
    matrices = transfer_level.astype(jnp.float32).reshape(2, 2, RANK, RANK)
    parent = jnp.einsum("iajbsr,abrt->ijst", blocks, matrices)
    return to_half(parent.reshape(span_rows, span_cols, SIDES * RANK))


def downward(parent, transfer_level):
    span_rows, span_cols = parent.shape[0], parent.shape[1]
    rounded = to_half(parent).astype(jnp.float32).reshape(span_rows, span_cols, SIDES, RANK)
    matrices = transfer_level.astype(jnp.float32).reshape(2, 2, RANK, RANK)
    child = jnp.einsum("ijst,abrt->iajbsr", rounded, matrices)
    return child.reshape(2 * span_rows, 2 * span_cols, SIDES * RANK)


def apply_operator(field, leaf_basis, transfer, coupling, near_table, near_mask, mask_leaf, mask_mid, mask_upper, mask_top):
    rows_all, cols_all = field.shape[0], field.shape[1]
    points = field.astype(jnp.float32).reshape(rows_all, cols_all, SIDES, LEAF)
    basis_mat = leaf_basis.astype(jnp.float32).reshape(rows_all, cols_all, LEAF, RANK)
    leaf_coeffs = to_half(jnp.einsum("ijsp,ijpr->ijsr", points, basis_mat).reshape(rows_all, cols_all, SIDES * RANK))
    mid_coeffs = upward(leaf_coeffs, transfer[0])
    upper_coeffs = upward(mid_coeffs, transfer[1])
    top_coeffs = upward(upper_coeffs, transfer[2])
    top_local = couple_whole(top_coeffs, mask_top, coupling[3])
    upper_local = couple_whole(upper_coeffs, mask_upper, coupling[2]) + downward(top_local, transfer[2])
    mid_local = couple_whole(mid_coeffs, mask_mid, coupling[1]) + downward(upper_local, transfer[1])
    leaf_local = couple_whole(leaf_coeffs, mask_leaf, coupling[0]) + downward(mid_local, transfer[0])
    padded_points = jnp.pad(points, ((1, 1), (1, 1), (0, 0), (0, 0)))
    near_mats = near_table.astype(jnp.float32).reshape(9, LEAF, LEAF)
    near = jnp.zeros((rows_all, cols_all, SIDES, LEAF), jnp.float32)
    for row_shift in range(3):
        for col_shift in range(3):
            source = padded_points[row_shift:row_shift + rows_all, col_shift:col_shift + cols_all]
            kept_mask = near_mask[:, :, row_shift * 3 + col_shift].astype(jnp.float32)
            near = near + jnp.einsum("ijsp,pq->ijsq", source * kept_mask[:, :, None, None], near_mats[row_shift * 3 + col_shift])
    leaf_half = to_half(leaf_local).astype(jnp.float32).reshape(rows_all, cols_all, SIDES, RANK)
    far_part = jnp.einsum("ijsr,ijpr->ijsp", leaf_half, basis_mat)
    return (near + far_part).reshape(rows_all, cols_all, SIDES * LEAF).astype(jnp.bfloat16)


def reference(sources, leaf_basis, transfer, coupling, near_table, near_mask, mask_leaf, mask_mid, mask_upper, mask_top):
    field = sources
    for product_step in range(PRODUCTS):
        field = apply_operator(field, leaf_basis, transfer, coupling, near_table, near_mask, mask_leaf, mask_mid, mask_upper, mask_top)
        field = lax.optimization_barrier(field)
    return field
```

```python
import functools

import jax
import jax.numpy as jnp
from jax import lax
from jax.experimental import pallas as pl
from jax.experimental.pallas import tpu as pltpu
from jax.sharding import PartitionSpec as P

LEAF = 64
RANK = 64
SIDES = 32
PRODUCTS = 3
PAIRS = SIDES // 2
WIDE = 2 * RANK
SLOTS = 27
ROW_AXES = ("rhs", "sub")
BF16 = jnp.bfloat16
F32 = jnp.float32


def window_slots(row_par, col_par):
    slots = []
    for a in range(6):
        for b in range(6):
            if abs(a - 2 - row_par) <= 1 and abs(b - 2 - col_par) <= 1:
                continue
            slots.append((a, b))
    return slots


def offset_index(slot, row_par, col_par):
    return 7 * (slot[0] + 1 - row_par) + slot[1] + 1 - col_par


CLASSES = [(row_par, col_par) for row_par in range(2) for col_par in range(2)]


def paired(matrices):
    zeros = jnp.zeros_like(matrices)
    upper = jnp.concatenate([matrices, zeros], -1)
    lower = jnp.concatenate([zeros, matrices], -1)
    return jnp.concatenate([upper, lower], -2)


def window_index(slot_mask, rows, cols):
    width = cols + 4
    zero_tile = (rows + 4) * width
    parts = []
    for row_par, col_par in CLASSES:
        slots = window_slots(row_par, col_par)
        first = jnp.asarray([a * width + b for a, b in slots], jnp.int32)
        row = jnp.arange(rows // 2, dtype=jnp.int32)[:, None, None] * (2 * width)
        col = jnp.arange(cols // 2, dtype=jnp.int32)[None, :, None] * 2
        kept = slot_mask[row_par::2, col_par::2] != 0
        parts.append(jnp.where(kept, row + col + first, zero_tile).reshape(-1))
    return parts


def near_index(near_mask, rows, cols):
    width = cols + 2
    first = jnp.asarray([u * width + v for u in range(3) for v in range(3)], jnp.int32)
    row = jnp.arange(rows, dtype=jnp.int32)[:, None, None] * width
    col = jnp.arange(cols, dtype=jnp.int32)[None, :, None]
    index = jnp.where(near_mask != 0, row + col + first, (rows + 2) * width)
    return [index[row_par::2, col_par::2].reshape(-1) for row_par, col_par in CLASSES]


def top_index(mask_top, row, count):
    parity = row % 2
    mask_row = lax.dynamic_slice_in_dim(mask_top, row, 1, 0)[0]
    place = [2, 3, 0, 1, 4, 5]
    tiles, tables = [], []
    for col_par in range(2):
        lists = [window_slots(row_par, col_par) for row_par in range(2)]
        a, b, o = [
            jnp.where(parity == 0, jnp.asarray(even, jnp.int32), jnp.asarray(odd, jnp.int32))
            for even, odd in (
                ([s[0] for s in lists[0]], [s[0] for s in lists[1]]),
                ([place[s[1]] for s in lists[0]], [place[s[1]] for s in lists[1]]),
                (
                    [offset_index(s, 0, col_par) for s in lists[0]],
                    [offset_index(s, 1, col_par) for s in lists[1]],
                ),
            )
        ]
        source = row - parity + a - 2
        kept = (mask_row[col_par] != 0) & (source >= 0) & (source < count)
        tiles.append(jnp.where(kept, source * 6 + b, 6 * count))
        tables.append(o)
    return tiles + tables


def dot(a, b):
    return jnp.dot(a, b, preferred_element_type=F32)


def dot_t(a, b):
    return lax.dot_general(a, b, (((1,), (1,)), ((), ())), preferred_element_type=F32)


def halves(ref):
    rows, cols = ref.shape[0], ref.shape[1]
    return ref.reshape(rows // 2, 2, cols // 2, 2, PAIRS, WIDE)


def tiles_of(value):
    return value.reshape(-1, WIDE)


def climb(child, parent, table, level):
    rows, cols = parent.shape[0], parent.shape[1]
    total = None
    for c, (a, b) in enumerate(CLASSES):
        block = tiles_of(halves(child)[:, a, :, b])
        part = dot(block, table[level, c])
        total = part if total is None else total + part
    parent[...] = total.astype(BF16).reshape(rows, cols, PAIRS, WIDE)


def upward_pass(field, basis, up_table, q0, q1, q2, q3, send_l, send_r, send_u, send_d):
    rows, cols = field.shape[0], field.shape[1]

    def leaf_row(i, carry):
        for j in range(cols):
            q0[i, j] = dot(field[i, j], basis[i * cols + j]).astype(BF16)
        return carry

    lax.fori_loop(0, rows, leaf_row, 0)
    climb(q0, q1, up_table, 0)
    climb(q1, q2, up_table, 1)
    climb(q2, q3, up_table, 2)
    for ref, side in ((send_l, 0), (send_r, 1)):
        at = 0
        for source, first, last, width in col_message(rows):
            level = (q0, q1, q2, q3, field)[source]
            low = 0 if side == 0 else level.shape[1] - width
            for r in range(first, last):
                ref[at : at + width] = level[r, low : low + width]
                at += width
    for ref, side in ((send_u, 0), (send_d, 1)):
        at = 0
        for level, width in ((q0, 2), (field, 1), (q1, 2), (q2, 2)):
            low = 0 if side == 0 else level.shape[0] - width
            for r in range(low, low + width):
                ref[at : at + level.shape[1]] = level[r]
                at += level.shape[1]


def col_message(rows):
    return [
        (0, 2, rows - 2, 2),
        (4, 1, rows - 1, 1),
        (0, 0, 2, 2),
        (4, 0, 1, 1),
        (1, 0, 2, 2),
        (2, 0, rows // 4, 2),
        (0, rows - 2, rows, 2),
        (4, rows - 1, rows, 1),
        (1, rows // 2 - 2, rows // 2, 2),
        (3, 0, rows // 8, 2),
    ]


def message_sizes(rows):
    counts = [(last - first) * width for _, first, last, width in col_message(rows)]
    start = sum(counts[:2])
    up = (start, start + sum(counts[2:6]))
    down = (start + sum(counts[2:5]), start + sum(counts[2:9]))
    return counts, up, down


def fill_windows(own, recv_l, recv_r, recv_u, recv_d, pads):
    q0, q1, q2, field = own
    p0, p1, p2, pf = pads
    rows = q0.shape[0]
    zero = jnp.zeros((PAIRS, WIDE), BF16)

    def place(level):
        ref, halo = {0: (p0, 2), 1: (p1, 2), 2: (p2, 2), 4: (pf, 1)}[level]
        source = {0: q0, 1: q1, 2: q2, 4: field}[level]
        return ref, halo, source.shape[0], source.shape[1]

    for level, source in ((0, q0), (1, q1), (2, q2), (4, field)):
        ref, halo, level_rows, level_cols = place(level)
        width = level_cols + 2 * halo
        ref[(level_rows + 2 * halo) * width] = zero
        for r in range(level_rows):
            start = (r + halo) * width + halo
            ref[start : start + level_cols] = source[r]
    for recv, side in ((recv_l, 0), (recv_r, 1)):
        at = 0
        for level, first, last, count in col_message(rows)[:-1]:
            ref, halo, level_rows, level_cols = place(level)
            width = level_cols + 2 * halo
            for r in range(first, last):
                start = (r + halo) * width + (0 if side == 0 else halo + level_cols)
                ref[start : start + count] = recv[at : at + count]
                at += count
    for recv, side in ((recv_u, 0), (recv_d, 1)):
        at = 0
        for level in (0, 4, 1, 2):
            ref, halo, level_rows, level_cols = place(level)
            width = level_cols + 2 * halo
            for r in range(halo):
                row = r if side == 0 else halo + level_rows + r
                start = row * width + halo
                ref[start : start + level_cols] = recv[at : at + level_cols]
                at += level_cols
        corner = (2, 0, 4, 1) if side == 0 else (0, 4, 1, 2)
        for edge in range(2):
            for level in corner:
                ref, halo, level_rows, level_cols = place(level)
                width = level_cols + 2 * halo
                for r in range(halo):
                    row = r if side == 0 else halo + level_rows + r
                    start = row * width + (0 if edge == 0 else halo + level_cols)
                    ref[start : start + halo] = recv[at : at + halo]
                    at += halo


def gather(index, base, count, slots, source, lhs):
    def one(n, carry):
        at = base + n * slots
        for k in range(slots):
            lhs[n, :, k * WIDE : (k + 1) * WIDE] = source[index[at + k]]
        return carry

    lax.fori_loop(0, count, one, 0)


def contract(lhs, count, tables, chunk=4):
    total = None
    for start in range(0, len(tables), chunk):
        group = tables[start : start + chunk]
        block = lhs[0:count, :, start * WIDE : (start + len(group)) * WIDE]
        weights = jnp.concatenate([read() for read in group], 0)
        part = dot(block.reshape(count * PAIRS, len(group) * WIDE), weights)
        total = part if total is None else total + part
    return total


def far_level(level, index, base, source, table, down_table, parent, lhs, out):
    rows, cols = out.shape[0], out.shape[1]
    count = rows * cols // 4
    for c, (row_par, col_par) in enumerate(CLASSES):
        slots = window_slots(row_par, col_par)
        gather(index, base + c * count * SLOTS, count, SLOTS, source, lhs)
        lhs[0:count, :, SLOTS * WIDE : (SLOTS + 1) * WIDE] = parent[...].reshape(
            count, PAIRS, WIDE
        )
        reads = [
            functools.partial(lambda o: table[o], offset_index(s, row_par, col_par)) for s in slots
        ]
        reads.append(functools.partial(lambda k: down_table[level, k], c))
        total = contract(lhs, count, reads)
        halves(out)[:, row_par, :, col_par] = total.astype(BF16).reshape(
            rows // 2, cols // 2, PAIRS, WIDE
        )


def product_kernel(last, sizes, *refs):
    (
        index, field, q0, q1, q2, column, recv_l, recv_r, recv_u, recv_d,
        tab0, tab1, tab2, tab3, up_table, down_table, near_table, basis,
    ) = refs[:18]
    outs = refs[18 : 19 if last else 27]
    p0, p1, p2, p3, pf, g0, g1, g2, g3, near, lhs = refs[19 if last else 27 :]
    rows, cols = field.shape[0], field.shape[1]
    count = column.shape[0]
    fill_windows((q0, q1, q2, field), recv_l, recv_r, recv_u, recv_d, (p0, p1, p2, pf))
    p3[0:count] = column[...]
    p3[count] = jnp.zeros((PAIRS, WIDE), BF16)
    base_near, base0, base1, base2, base3, base_top = sizes
    for j in range(2):
        for k in range(SLOTS):
            lhs[0, :, k * WIDE : (k + 1) * WIDE] = p3[index[base3 + j * SLOTS + k]]
        reads = [
            functools.partial(lambda k: tab3[index[k]], base_top + j * SLOTS + k)
            for k in range(SLOTS)
        ]
        g3[0, j] = contract(lhs, 1, reads).astype(BF16)
    far_level(2, index, base2, p2, tab2, down_table, g3, lhs, g2)
    far_level(1, index, base1, p1, tab1, down_table, g2, lhs, g1)
    far_level(0, index, base0, p0, tab0, down_table, g1, lhs, g0)
    quarter = rows * cols // 4
    for c, (row_par, col_par) in enumerate(CLASSES):
        gather(index, base_near + c * quarter * 9, quarter, 9, pf, lhs)
        reads = [functools.partial(lambda k: near_table[k], k) for k in range(9)]
        total = contract(lhs, quarter, reads)
        halves(near)[:, row_par, :, col_par] = total.reshape(rows // 2, cols // 2, PAIRS, WIDE)
    result = outs[0]

    def leaf_row(i, carry):
        for j in range(cols):
            far = dot_t(g0[i, j], basis[i * cols + j])
            result[i, j] = (near[i, j] + far).astype(BF16)
        return carry

    lax.fori_loop(0, rows, leaf_row, 0)
    if not last:
        upward_pass(result, basis, up_table, *outs[1:])


def first_kernel(field, basis, up_table, *outs):
    upward_pass(field, basis, up_table, *outs)


def shape_of(*dims):
    return jax.ShapeDtypeStruct(tuple(dims) + (PAIRS, WIDE), BF16)


def upward_shapes(rows, cols):
    counts, _, _ = message_sizes(rows)
    edge = 2 * cols + cols + cols + cols // 2
    return [
        shape_of(rows, cols),
        shape_of(rows // 2, cols // 2),
        shape_of(rows // 4, cols // 4),
        shape_of(rows // 8, cols // 8),
        shape_of(sum(counts)),
        shape_of(sum(counts)),
        shape_of(edge),
        shape_of(edge),
    ]


VMEM = pl.BlockSpec(memory_space=pltpu.VMEM)
SMEM = pl.BlockSpec(memory_space=pltpu.SMEM)
PARAMS = pltpu.CompilerParams(vmem_limit_bytes=48 * 1024 * 1024)


def start_up(field, basis, up_table):
    outs = upward_shapes(field.shape[0], field.shape[1])
    return pl.pallas_call(
        first_kernel,
        out_shape=outs,
        in_specs=[VMEM] * 3,
        out_specs=[VMEM] * len(outs),
        compiler_params=PARAMS,
    )(field, basis, up_table)


def product(last, sizes, index, field, q0, q1, q2, column, received, tables):
    rows, cols = field.shape[0], field.shape[1]
    outs = [shape_of(rows, cols)]
    if not last:
        outs += upward_shapes(rows, cols)

    def tile_scratch(*dims):
        return pltpu.VMEM(tuple(dims) + (PAIRS, WIDE), BF16)

    args = (index, field, q0, q1, q2, column, *received, *tables)
    result = pl.pallas_call(
        functools.partial(product_kernel, last, sizes),
        out_shape=outs,
        in_specs=[SMEM] + [VMEM] * (len(args) - 1),
        out_specs=[VMEM] * len(outs),
        scratch_shapes=[
            tile_scratch((rows + 4) * (cols + 4) + 1),
            tile_scratch((rows // 2 + 4) * (cols // 2 + 4) + 1),
            tile_scratch((rows // 4 + 4) * (cols // 4 + 4) + 1),
            tile_scratch(column.shape[0] + 1),
            tile_scratch((rows + 2) * (cols + 2) + 1),
            tile_scratch(rows, cols),
            tile_scratch(rows // 2, cols // 2),
            tile_scratch(rows // 4, cols // 4),
            tile_scratch(rows // 8, cols // 8),
            pltpu.VMEM((rows, cols, PAIRS, WIDE), F32),
            pltpu.VMEM((rows * cols // 4, PAIRS, (SLOTS + 1) * WIDE), BF16),
        ],
        compiler_params=PARAMS,
    )(*args)
    return result


def shift(value, axis, step):
    count = lax.axis_size(axis)
    pairs = [(i, i + step) for i in range(count) if 0 <= i + step < count]
    return lax.ppermute(value, axis, pairs)


def exchange(rows, q3, send_l, send_r, send_u, send_d):
    counts, up, down = message_sizes(rows)
    recv_l = shift(send_r, "br", 1)
    recv_r = shift(send_l, "br", -1)
    up_message = jnp.concatenate([send_u, recv_l[up[0] : up[1]], recv_r[up[0] : up[1]]], 0)
    down_message = jnp.concatenate(
        [send_d, recv_l[down[0] : down[1]], recv_r[down[0] : down[1]]], 0
    )
    recv_d = shift(up_message, ROW_AXES, -1)
    recv_u = shift(down_message, ROW_AXES, 1)
    last = down[1]
    wide = jnp.concatenate([q3[0], recv_l[last:], recv_r[last:]], 0)
    column = lax.all_gather(wide, ROW_AXES, axis=0, tiled=True)
    return column, (recv_l, recv_r, recv_u, recv_d)


def on_device(
    sources, leaf_basis, transfer, coupling, near_table, near_mask,
    mask_leaf, mask_mid, mask_upper, mask_top,
):
    rows, cols = sources.shape[0], sources.shape[1]
    row = lax.axis_index(ROW_AXES)
    row_count = lax.axis_size(ROW_AXES)
    field = sources.reshape(rows, cols, PAIRS, WIDE)
    basis = paired(leaf_basis.reshape(rows * cols, LEAF, RANK))
    tables = paired(coupling.reshape(4, 49, RANK, RANK))
    moves = transfer.reshape(3, 4, RANK, RANK)
    up_table = paired(moves)
    down_table = paired(jnp.swapaxes(moves, 2, 3))
    near_pair = paired(near_table.reshape(9, LEAF, LEAF))
    upper = lax.dynamic_slice_in_dim(mask_upper, row * (rows // 4), rows // 4, 0)
    lists = [
        near_index(near_mask, rows, cols),
        window_index(mask_leaf, rows, cols),
        window_index(mask_mid, rows // 2, cols // 2),
        window_index(upper, rows // 4, cols // 4),
    ]
    top = top_index(mask_top, row, row_count)
    lists += [top[:2], top[2:]]
    bases, at = [], 0
    for group in lists:
        bases.append(at)
        at += sum(part.shape[0] for part in group)
    index = jnp.concatenate([part for group in lists for part in group], 0)
    tabs = (tables[0], tables[1], tables[2], tables[3], up_table, down_table, near_pair, basis)
    q0, q1, q2, q3, *sends = start_up(field, basis, up_table)
    for step in range(PRODUCTS):
        column, received = exchange(rows, q3, *sends)
        last = step == PRODUCTS - 1
        outs = product(last, tuple(bases), index, field, q0, q1, q2, column, received, tabs)
        field = outs[0]
        if not last:
            q0, q1, q2, q3, *sends = outs[1:]
    return field.reshape(rows, cols, SIDES * LEAF)


def solution(mesh):
    placed = (
        P(("grp", "rhs", "sub"), "br", None),
        P(("grp", "rhs", "sub"), "br", None),
        P(),
        P(),
        P(),
        P(("grp", "rhs", "sub"), "br", None),
        P(("grp", "rhs", "sub"), "br", None),
        P(("grp", "rhs", "sub"), "br", None),
        P("grp", "br", None),
        P("grp", "br", None),
    )
    return jax.shard_map(
        on_device,
        mesh=mesh,
        in_specs=placed,
        out_specs=P(("grp", "rhs", "sub"), "br", None),
        check_vma=False,
    )
```

```python
import functools

import jax
import jax.numpy as jnp
from jax import lax
from jax.experimental import pallas as pl
from jax.experimental.pallas import tpu as pltpu
from jax.sharding import PartitionSpec as P

LEAF = 64
RANK = 64
SIDES = 32
PRODUCTS = 3
PAIRS = SIDES // 2
WIDE = 2 * RANK
SLOTS = 27
ROW_AXES = ("rhs", "sub")
UP_AT = 4 * 49
NEAR_AT = UP_AT + 12
DOWN_AT = NEAR_AT + 10
BF16 = jnp.bfloat16
F32 = jnp.float32


def window_slots(row_par, col_par):
    slots = []
    for a in range(6):
        for b in range(6):
            if abs(a - 2 - row_par) <= 1 and abs(b - 2 - col_par) <= 1:
                continue
            slots.append((a, b))
    return slots


def offset_index(slot, row_par, col_par):
    return 7 * (slot[0] + 1 - row_par) + slot[1] + 1 - col_par


CLASSES = [(row_par, col_par) for row_par in range(2) for col_par in range(2)]


def top_index(mask_top, row, count, place_row):
    parity = row % 2
    mask_row = lax.dynamic_slice_in_dim(mask_top, row, 1, 0)[0]
    place = [2, 3, 0, 1, 4, 5]
    tiles, tables = [], []
    for col_par in range(2):
        lists = [window_slots(row_par, col_par) for row_par in range(2)]
        a, b, o = [
            jnp.where(parity == 0, jnp.asarray(even, jnp.int32), jnp.asarray(odd, jnp.int32))
            for even, odd in (
                ([s[0] for s in lists[0]], [s[0] for s in lists[1]]),
                ([place[s[1]] for s in lists[0]], [place[s[1]] for s in lists[1]]),
                (
                    [offset_index(s, 0, col_par) for s in lists[0]],
                    [offset_index(s, 1, col_par) for s in lists[1]],
                ),
            )
        ]
        source = row - parity + a - 2
        kept = (mask_row[col_par] != 0) & (source >= 0) & (source < count)
        tiles.append(jnp.where(kept, place_row(source) * 6 + b, 6 * count))
        tables.append(o)
    return tiles + tables


def dot(a, b):
    return jnp.dot(a, b, preferred_element_type=F32)


def dot_t(a, b):
    return lax.dot_general(a, b, (((1,), (1,)), ((), ())), preferred_element_type=F32)


def halves(ref):
    rows, cols = ref.shape[0], ref.shape[1]
    return ref.reshape(rows // 2, 2, cols // 2, 2, PAIRS, WIDE)


def tiles_of(value):
    return value.reshape(-1, WIDE)


def climb(child, parent, table, first):
    rows, cols = parent.shape[0], parent.shape[1]
    total = None
    for c, (a, b) in enumerate(CLASSES):
        block = tiles_of(halves(child)[:, a, :, b])
        part = dot(block, table[first + c])
        total = part if total is None else total + part
    parent[...] = total.astype(BF16).reshape(rows, cols, PAIRS, WIDE)


def upward_pass(field, basis, table, first, q0, q1, q2, q3, send_l, send_r, send_u, send_d):
    rows, cols = field.shape[0], field.shape[1]

    def leaf_row(i, carry):
        for j in range(cols):
            q0[i, j] = dot(field[i, j], basis[i * cols + j]).astype(BF16)
        return carry

    lax.fori_loop(0, rows, leaf_row, 0)
    climb(q0, q1, table, first + 0)
    climb(q1, q2, table, first + 4)
    climb(q2, q3, table, first + 8)
    for ref, side in ((send_l, 0), (send_r, 1)):
        at = 0
        for source, first, last, width in col_message(rows):
            level = (q0, q1, q2, q3, field)[source]
            low = 0 if side == 0 else level.shape[1] - width
            for r in range(first, last):
                ref[at : at + width] = level[r, low : low + width]
                at += width
    for ref, side in ((send_u, 0), (send_d, 1)):
        at = 0
        for level, width in ((q0, 2), (field, 1), (q1, 2), (q2, 2)):
            low = 0 if side == 0 else level.shape[0] - width
            for r in range(low, low + width):
                ref[at : at + level.shape[1]] = level[r]
                at += level.shape[1]


def col_message(rows):
    return [
        (0, 2, rows - 2, 2),
        (4, 1, rows - 1, 1),
        (0, 0, 2, 2),
        (4, 0, 1, 1),
        (1, 0, 2, 2),
        (2, 0, rows // 4, 2),
        (0, rows - 2, rows, 2),
        (4, rows - 1, rows, 1),
        (1, rows // 2 - 2, rows // 2, 2),
        (3, 0, rows // 8, 2),
    ]


def message_sizes(rows):
    counts = [(last - first) * width for _, first, last, width in col_message(rows)]
    start = sum(counts[:2])
    up = (start, start + sum(counts[2:6]))
    down = (start + sum(counts[2:5]), start + sum(counts[2:9]))
    return counts, up, down


def fill_windows(own, recv_l, recv_r, recv_u, recv_d, pads):
    q0, q1, q2, field = own
    p0, p1, p2, pf = pads
    rows = q0.shape[0]

    def place(level):
        ref, halo = {0: (p0, 2), 1: (p1, 2), 2: (p2, 2), 4: (pf, 1)}[level]
        source = {0: q0, 1: q1, 2: q2, 4: field}[level]
        return ref, halo, source.shape[0], source.shape[1]

    for level, source in ((0, q0), (1, q1), (2, q2), (4, field)):
        ref, halo, level_rows, level_cols = place(level)
        width = level_cols + 2 * halo
        for r in range(level_rows):
            start = (r + halo) * width + halo
            ref[start : start + level_cols] = source[r]
    for recv, side in ((recv_l, 0), (recv_r, 1)):
        at = 0
        for level, first, last, count in col_message(rows)[:-1]:
            ref, halo, level_rows, level_cols = place(level)
            width = level_cols + 2 * halo
            for r in range(first, last):
                start = (r + halo) * width + (0 if side == 0 else halo + level_cols)
                ref[start : start + count] = recv[at : at + count]
                at += count
    for recv, side in ((recv_u, 0), (recv_d, 1)):
        at = 0
        for level in (0, 4, 1, 2):
            ref, halo, level_rows, level_cols = place(level)
            width = level_cols + 2 * halo
            for r in range(halo):
                row = r if side == 0 else halo + level_rows + r
                start = row * width + halo
                ref[start : start + level_cols] = recv[at : at + level_cols]
                at += level_cols
        corner = (2, 0, 4, 1) if side == 0 else (0, 4, 1, 2)
        for edge in range(2):
            for level in corner:
                ref, halo, level_rows, level_cols = place(level)
                width = level_cols + 2 * halo
                for r in range(halo):
                    row = r if side == 0 else halo + level_rows + r
                    start = row * width + (0 if edge == 0 else halo + level_cols)
                    ref[start : start + halo] = recv[at : at + halo]
                    at += halo


def contract(lhs, count, tables, chunk=4):
    total = None
    for start in range(0, len(tables), chunk):
        group = tables[start : start + chunk]
        block = lhs[0:count, :, start * WIDE : (start + len(group)) * WIDE]
        weights = jnp.concatenate([read() for read in group], 0)
        part = dot(block.reshape(count * PAIRS, len(group) * WIDE), weights)
        total = part if total is None else total + part
    return total


def masked(tiles, words, bit):
    parts = []
    for n, (i, j) in enumerate(words[1]):
        kept = jnp.bitwise_and(words[0][i, j : j + 1, :], jnp.int32(1 << bit)) != 0
        kept = jnp.broadcast_to(kept, (PAIRS, WIDE))
        parts.append(jnp.where(kept, tiles[n], jnp.zeros((), BF16)))
    return jnp.concatenate(parts, 0)


def windows_dot(reads, words, table, extra=None):
    total = None
    for start in range(0, len(reads), 2):
        group = list(enumerate(reads))[start : start + 2]
        blocks = [masked(read(), words, k) for k, (read, _) in group]
        weights = [table[at] for _, (_, at) in group]
        if extra is not None and len(group) == 1:
            blocks.append(extra[0])
            weights.append(extra[1])
        part = dot(jnp.concatenate(blocks, 1), jnp.concatenate(weights, 0))
        total = part if total is None else total + part
    return total


def far_level(level, words, padded, table, parent, out):
    rows, cols = out.shape[0], out.shape[1]
    half_rows, half_cols = rows // 2, cols // 2
    grid = padded.reshape(half_rows + 2, 2, half_cols + 2, 2, PAIRS, WIDE)
    for c, (row_par, col_par) in enumerate(CLASSES):
        spots = [
            (2 * i + row_par, 2 * j + col_par) for i in range(half_rows) for j in range(half_cols)
        ]

        def read(a, b):
            value = grid[a // 2 : a // 2 + half_rows, a % 2, b // 2 : b // 2 + half_cols, b % 2]
            return value.reshape(half_rows * half_cols, PAIRS, WIDE)

        reads = [
            (
                functools.partial(read, slot[0], slot[1]),
                49 * level + offset_index(slot, row_par, col_par),
            )
            for slot in window_slots(row_par, col_par)
        ]
        extra = (tiles_of(parent[...]), table[DOWN_AT + 4 * level + c])
        total = windows_dot(reads, (words, spots), table, extra)
        halves(out)[:, row_par, :, col_par] = total.astype(BF16).reshape(
            half_rows, half_cols, PAIRS, WIDE
        )


def product_kernel(last, row_tiles, *refs):
    (
        index, words_near, words0, words1, words2, field, q0, q1, q2, column,
        recv_l, recv_r, recv_u, recv_d, table, basis,
    ) = refs[:16]
    outs = refs[16 : 17 if last else 25]
    p0, p1, p2, p3, pf, g0, g1, g2, g3, near, lhs = refs[17 if last else 25 :]
    rows, cols = field.shape[0], field.shape[1]
    count = column.shape[0]
    fill_windows((q0, q1, q2, field), recv_l, recv_r, recv_u, recv_d, (p0, p1, p2, pf))
    p3[0:count] = column[...]
    p3[count] = jnp.zeros((PAIRS, WIDE), BF16)
    for j in range(2):
        for k in range(SLOTS):
            lhs[0, :, k * WIDE : (k + 1) * WIDE] = p3[index[j * SLOTS + k]]
        reads = [
            functools.partial(lambda k: table[3 * 49 + index[k]], (2 + j) * SLOTS + k)
            for k in range(SLOTS)
        ]
        g3[0, j] = contract(lhs, 1, reads).astype(BF16)
    far_level(2, words2, p2, table, g3, g2)
    far_level(1, words1, p1, table, g2, g1)
    far_level(0, words0, p0, table, g1, g0)
    grid = pf.reshape(rows + 2, cols + 2, PAIRS, WIDE)
    for top in range(0, rows, row_tiles):

        def read(u, v):
            value = grid[top + u : top + u + row_tiles, v : v + cols]
            return value.reshape(row_tiles * cols, PAIRS, WIDE)

        spots = [(top + i, j) for i in range(row_tiles) for j in range(cols)]
        reads = [
            (functools.partial(read, u, v), NEAR_AT + 3 * u + v) for u in range(3) for v in range(3)
        ]
        total = windows_dot(reads, (words_near, spots), table)
        near[top : top + row_tiles] = total.reshape(row_tiles, cols, PAIRS, WIDE)
    result = outs[0]

    def leaf_row(i, carry):
        for j in range(cols):
            far = dot_t(g0[i, j], basis[i * cols + j])
            result[i, j] = (near[i, j] + far).astype(BF16)
        return carry

    lax.fori_loop(0, rows, leaf_row, 0)
    if not last:
        upward_pass(result, basis, table, UP_AT, *outs[1:])


def half_lanes(rows):
    return lax.broadcasted_iota(jnp.int32, (rows, WIDE), 1) < WIDE // 2


def expand_pair(first, second, order):
    low = half_lanes(RANK // 2)
    one, two = first.astype(F32), second.astype(F32)
    upper = jnp.where(low, one, pltpu.roll(two, WIDE // 2, 1))
    lower = jnp.where(low, pltpu.roll(one, WIDE // 2, 1), two)
    both = dot(order, jnp.concatenate([upper, lower], 0).astype(BF16))
    turned = pltpu.roll(both, WIDE // 2, 1)
    low = half_lanes(RANK)
    zero = jnp.zeros((), F32)
    blocks = [
        (jnp.where(low, both, zero), jnp.where(low, zero, turned)),
        (jnp.where(low, turned, zero), jnp.where(low, zero, both)),
    ]
    return [jnp.concatenate(pair, 0) for pair in blocks]


def row_order():
    to = lax.broadcasted_iota(jnp.int32, (RANK, RANK), 0)
    source = lax.broadcasted_iota(jnp.int32, (RANK, RANK), 1)
    return (source == (to % 2) * (RANK // 2) + to // 2).astype(F32).astype(BF16)


def expand(packed, out, count, unroll):
    order = row_order()

    def some(n, carry):
        for k in range(unroll):
            at = 2 * (n * unroll + k)
            one, two = expand_pair(packed[at], packed[at + 1], order)
            out[at] = one.astype(BF16)
            out[at + 1] = two.astype(BF16)
        return carry

    steps = count // 2 // unroll
    lax.fori_loop(0, steps, some, 0)
    for at in range(2 * unroll * steps, count, 2):
        one, two = expand_pair(packed[at], packed[at + 1], order)
        out[at] = one.astype(BF16)
        out[at + 1] = two.astype(BF16)


def first_kernel(field, packed_basis, packed_up, basis, *rest):
    outs, up_table = rest[:-1], rest[-1]
    expand(packed_basis, basis, packed_basis.shape[0], 8)
    expand(packed_up, up_table, packed_up.shape[0], 6)
    upward_pass(field, basis, up_table, 0, *outs)


def mask_words(mask, out):
    slots = mask.shape[2]
    slot = lax.broadcasted_iota(jnp.int32, (slots, WIDE), 0)

    def powers(low, high):
        value = jnp.where((slot >= low) & (slot < high), jnp.left_shift(1, slot - low), 0)
        return value.astype(F32).astype(BF16)

    for i in range(mask.shape[0]):
        row = (mask[i] != 0).astype(F32).astype(BF16)
        word = dot(row, powers(0, min(14, slots))).astype(jnp.int32)
        if slots > 14:
            word = word + jnp.left_shift(dot(row, powers(14, slots)).astype(jnp.int32), 14)
        out[i] = word


def table_kernel(packed, near_mask, mask0, mask1, mask2, table, *words):
    expand(packed, table, packed.shape[0], 6)
    for k in range(12):
        wide = table[UP_AT + k].astype(F32)
        table[DOWN_AT + k] = jnp.swapaxes(wide, 0, 1).astype(BF16)
    for mask, out in zip((near_mask, mask0, mask1, mask2), words):
        mask_words(mask, out)


def shape_of(*dims):
    return jax.ShapeDtypeStruct(tuple(dims) + (PAIRS, WIDE), BF16)


def upward_shapes(rows, cols):
    counts, _, _ = message_sizes(rows)
    edge = 2 * cols + cols + cols + cols // 2
    return [
        shape_of(rows, cols),
        shape_of(rows // 2, cols // 2),
        shape_of(rows // 4, cols // 4),
        shape_of(rows // 8, cols // 8),
        shape_of(sum(counts)),
        shape_of(sum(counts)),
        shape_of(edge),
        shape_of(edge),
    ]


VMEM = pl.BlockSpec(memory_space=pltpu.VMEM)
SMEM = pl.BlockSpec(memory_space=pltpu.SMEM)
PARAMS = pltpu.CompilerParams(vmem_limit_bytes=24 * 1024 * 1024)


def start_up(field, packed_basis, packed_up):
    rows, cols = field.shape[0], field.shape[1]
    outs = [jax.ShapeDtypeStruct((rows * cols, WIDE, WIDE), BF16)]
    outs += upward_shapes(rows, cols)
    return pl.pallas_call(
        first_kernel,
        out_shape=outs,
        in_specs=[VMEM] * 3,
        out_specs=[VMEM] * len(outs),
        scratch_shapes=[pltpu.VMEM((12, WIDE, WIDE), BF16)],
        compiler_params=PARAMS,
    )(field, packed_basis, packed_up)


def build_tables(packed, masks):
    outs = [jax.ShapeDtypeStruct((packed.shape[0] + 12, WIDE, WIDE), BF16)]
    outs += [jax.ShapeDtypeStruct(mask.shape[:2] + (WIDE,), jnp.int32) for mask in masks]
    return pl.pallas_call(
        table_kernel,
        out_shape=outs,
        in_specs=[VMEM] * 5,
        out_specs=[VMEM] * 5,
        compiler_params=PARAMS,
    )(packed, *masks)


def product(last, index, words, field, q0, q1, q2, column, received, table, basis):
    rows, cols = field.shape[0], field.shape[1]
    outs = [shape_of(rows, cols)]
    if not last:
        outs += upward_shapes(rows, cols)

    def tile_scratch(*dims):
        return pltpu.VMEM(tuple(dims) + (PAIRS, WIDE), BF16)

    args = (index, *words, field, q0, q1, q2, column, *received, table, basis)
    return pl.pallas_call(
        functools.partial(product_kernel, last, 2),
        out_shape=outs,
        in_specs=[SMEM] + [VMEM] * (len(args) - 1),
        out_specs=[VMEM] * len(outs),
        scratch_shapes=[
            tile_scratch((rows + 4) * (cols + 4)),
            tile_scratch((rows // 2 + 4) * (cols // 2 + 4)),
            tile_scratch((rows // 4 + 4) * (cols // 4 + 4)),
            tile_scratch(column.shape[0] + 1),
            tile_scratch((rows + 2) * (cols + 2)),
            tile_scratch(rows, cols),
            tile_scratch(rows // 2, cols // 2),
            tile_scratch(rows // 4, cols // 4),
            tile_scratch(rows // 8, cols // 8),
            pltpu.VMEM((rows, cols, PAIRS, WIDE), F32),
            pltpu.VMEM((1, PAIRS, SLOTS * WIDE), BF16),
        ],
        compiler_params=PARAMS,
    )(*args)


def shift(value, axis, step):
    count = lax.axis_size(axis)
    pairs = [(i, i + step) for i in range(count) if 0 <= i + step < count]
    return lax.ppermute(value, axis, pairs)


def two_by_two():
    return lax.axis_size("rhs") == 2 and lax.axis_size("sub") == 2


def exchange(rows, q3, send_l, send_r, send_u, send_d):
    counts, up, down = message_sizes(rows)
    recv_l = shift(send_r, "br", 1)
    recv_r = shift(send_l, "br", -1)
    last = down[1]
    wide = jnp.concatenate([q3[0], recv_l[last:], recv_r[last:]], 0)
    tail = []
    swap = [(0, 1), (1, 0)]
    if two_by_two():
        tail = [wide, lax.ppermute(wide, "sub", swap)]
    up_message = jnp.concatenate([send_u, recv_l[up[0] : up[1]], recv_r[up[0] : up[1]], *tail], 0)
    down_message = jnp.concatenate(
        [send_d, recv_l[down[0] : down[1]], recv_r[down[0] : down[1]], *tail], 0
    )
    recv_d = shift(up_message, ROW_AXES, -1)
    recv_u = shift(down_message, ROW_AXES, 1)
    if two_by_two():
        start = up_message.shape[0] - 2 * wide.shape[0]
        mine = jnp.where(lax.axis_index("sub") == 1, recv_d[start:], recv_u[start:])
        far = mine + lax.ppermute(mine, "sub", swap)
        column = jnp.concatenate([*tail, far], 0)
    else:
        column = lax.all_gather(wide, ROW_AXES, axis=0, tiled=True)
    return column, (recv_l, recv_r, recv_u, recv_d)


def column_place(source):
    if not two_by_two():
        return source
    rhs, sub = lax.axis_index("rhs"), lax.axis_index("sub")
    inner = source % 2
    near_place = jnp.where(inner == sub, 0, 1)
    far_place = jnp.where(inner == rhs, 2, 3)
    return jnp.where(source // 2 == rhs, near_place, far_place)


def on_device(
    sources, leaf_basis, transfer, coupling, near_table, near_mask,
    mask_leaf, mask_mid, mask_upper, mask_top,
):
    rows, cols = sources.shape[0], sources.shape[1]
    row = lax.axis_index(ROW_AXES)
    row_count = lax.axis_size(ROW_AXES)
    field = sources.reshape(rows, cols, PAIRS, WIDE)
    packed_basis = leaf_basis.reshape(rows * cols, LEAF // 2, WIDE)
    moves = transfer.reshape(12, RANK * RANK)
    packed_up = moves.reshape(12, RANK // 2, WIDE)
    basis, q0, q1, q2, q3, *sends = start_up(field, packed_basis, packed_up)
    filler = jnp.zeros((1, RANK * RANK), BF16)
    packed = jnp.concatenate([coupling.reshape(4 * 49, RANK * RANK), moves, near_table, filler], 0)
    packed = packed.reshape(DOWN_AT, RANK // 2, WIDE)
    upper = lax.dynamic_slice_in_dim(mask_upper, row * (rows // 4), rows // 4, 0)
    table, *words = build_tables(packed, (near_mask, mask_leaf, mask_mid, upper))
    index = jnp.concatenate(top_index(mask_top, row, row_count, column_place), 0)
    for step in range(PRODUCTS):
        column, received = exchange(rows, q3, *sends)
        last = step == PRODUCTS - 1
        outs = product(last, index, words, field, q0, q1, q2, column, received, table, basis)
        field = outs[0]
        if not last:
            q0, q1, q2, q3, *sends = outs[1:]
    return field.reshape(rows, cols, SIDES * LEAF)


def solution(mesh):
    placed = (
        P(("grp", "rhs", "sub"), "br", None),
        P(("grp", "rhs", "sub"), "br", None),
        P(),
        P(),
        P(),
        P(("grp", "rhs", "sub"), "br", None),
        P(("grp", "rhs", "sub"), "br", None),
        P(("grp", "rhs", "sub"), "br", None),
        P("grp", "br", None),
        P("grp", "br", None),
    )
    return jax.shard_map(
        on_device,
        mesh=mesh,
        in_specs=placed,
        out_specs=P(("grp", "rhs", "sub"), "br", None),
        check_vma=False,
    )
```

```python
import functools

import jax
import jax.numpy as jnp
from jax import lax
from jax.experimental import pallas as pl
from jax.experimental.pallas import tpu as pltpu
from jax.sharding import PartitionSpec as P

LEAF = 64
RANK = 64
SIDES = 32
PRODUCTS = 3
PAIRS = SIDES // 2
WIDE = 2 * RANK
SLOTS = 27
ROW_AXES = ("rhs", "sub")
UP_AT = 4 * 49
NEAR_AT = UP_AT + 12
DOWN_AT = NEAR_AT + 9
BF16 = jnp.bfloat16
F32 = jnp.float32


def window_slots(row_par, col_par):
    slots = []
    for a in range(6):
        for b in range(6):
            if abs(a - 2 - row_par) <= 1 and abs(b - 2 - col_par) <= 1:
                continue
            slots.append((a, b))
    return slots


def offset_index(slot, row_par, col_par):
    return 7 * (slot[0] + 1 - row_par) + slot[1] + 1 - col_par


CLASSES = [(row_par, col_par) for row_par in range(2) for col_par in range(2)]


def top_entry(place, mask, col_par, k, count):
    row, rhs, sub, folded = place[0], place[1], place[2], place[3]
    parity = jnp.bitwise_and(row, 1)
    even, odd = [window_slots(row_par, col_par)[k] for row_par in range(2)]
    spots = [2, 3, 0, 1, 4, 5]

    def pick(first, second):
        return jnp.where(parity == 0, jnp.int32(first), jnp.int32(second))

    source = row - parity + pick(even[0], odd[0]) - 2
    inner = jnp.bitwise_and(source, 1)
    near_place = jnp.where(inner == sub, 0, 1)
    far_place = jnp.where(inner == rhs, 2, 3)
    two = jnp.where(jnp.right_shift(source, 1) == rhs, near_place, far_place)
    at = jnp.where(folded == 1, two, source)
    kept = (mask[row, col_par, k] != 0) & (source >= 0) & (source < count)
    tile = jnp.where(kept, at * 6 + pick(spots[even[1]], spots[odd[1]]), 6 * count)
    return tile, pick(offset_index(even, 0, col_par), offset_index(odd, 1, col_par))


def dot(a, b):
    return jnp.dot(a, b, preferred_element_type=F32)


def dot_t(a, b):
    return lax.dot_general(a, b, (((1,), (1,)), ((), ())), preferred_element_type=F32)


def halves(ref):
    rows, cols = ref.shape[0], ref.shape[1]
    return ref.reshape(rows // 2, 2, cols // 2, 2, PAIRS, WIDE)


def tiles_of(value):
    return value.reshape(-1, WIDE)


def climb(child, parent, table, first):
    rows, cols = parent.shape[0], parent.shape[1]
    total = None
    for c, (a, b) in enumerate(CLASSES):
        block = tiles_of(halves(child)[:, a, :, b])
        part = dot(block, table[first + c])
        total = part if total is None else total + part
    parent[...] = total.astype(BF16).reshape(rows, cols, PAIRS, WIDE)


def upward_pass(field, basis, table, first, q0, q1, q2, q3, send_l, send_r, send_u, send_d):
    rows, cols = field.shape[0], field.shape[1]

    def leaf_rows(step, carry):
        for part in range(2):
            i = 2 * step + part
            for j in range(cols):
                q0[i, j] = dot(field[i, j], basis[i * cols + j]).astype(BF16)
        return carry

    lax.fori_loop(0, rows // 2, leaf_rows, 0)
    climb(q0, q1, table, first + 0)
    climb(q1, q2, table, first + 4)
    climb(q2, q3, table, first + 8)
    for ref, side in ((send_l, 0), (send_r, 1)):
        at = 0
        for source, first, last, width in col_message(rows):
            level = (q0, q1, q2, q3, field)[source]
            low = 0 if side == 0 else level.shape[1] - width
            for r in range(first, last):
                ref[at : at + width] = level[r, low : low + width]
                at += width
    for ref, side in ((send_u, 0), (send_d, 1)):
        at = 0
        for level, width in ((q0, 2), (field, 1), (q1, 2), (q2, 2)):
            low = 0 if side == 0 else level.shape[0] - width
            for r in range(low, low + width):
                ref[at : at + level.shape[1]] = level[r]
                at += level.shape[1]


def col_message(rows):
    return [
        (0, 2, rows - 2, 2),
        (4, 1, rows - 1, 1),
        (0, 0, 2, 2),
        (4, 0, 1, 1),
        (1, 0, 2, 2),
        (2, 0, rows // 4, 2),
        (0, rows - 2, rows, 2),
        (4, rows - 1, rows, 1),
        (1, rows // 2 - 2, rows // 2, 2),
        (3, 0, rows // 8, 2),
    ]


def message_sizes(rows):
    counts = [(last - first) * width for _, first, last, width in col_message(rows)]
    start = sum(counts[:2])
    up = (start, start + sum(counts[2:6]))
    down = (start + sum(counts[2:5]), start + sum(counts[2:9]))
    return counts, up, down


def fill_windows(own, recv_l, recv_r, pads):
    q0, q1, q2, field = own
    p0, p1, p2, pf = pads
    rows = q0.shape[0]
    levels = {0: (p0, 2, q0), 1: (p1, 2, q1), 2: (p2, 2, q2), 4: (pf, 1, field)}
    for ref, halo, source in levels.values():
        level_rows, level_cols = source.shape[0], source.shape[1]
        width = level_cols + 2 * halo
        blank = jnp.zeros((halo * width, PAIRS, WIDE), BF16)
        ref[0 : halo * width] = blank
        ref[(halo + level_rows) * width : (2 * halo + level_rows) * width] = blank
        for r in range(level_rows):
            start = (r + halo) * width + halo
            ref[start : start + level_cols] = source[r]
    for recv, side in ((recv_l, 0), (recv_r, 1)):
        at = 0
        for level, first, last, count in col_message(rows)[:-1]:
            ref, halo, source = levels[level]
            level_cols = source.shape[1]
            width = level_cols + 2 * halo
            for r in range(first, last):
                start = (r + halo) * width + (0 if side == 0 else halo + level_cols)
                ref[start : start + count] = recv[at : at + count]
                at += count


def fill_edges(cols, recv, pads, side):
    p0, p1, p2, pf = pads
    levels = {0: (p0, 2, cols), 4: (pf, 1, cols), 1: (p1, 2, cols // 2), 2: (p2, 2, cols // 4)}
    at = 0
    for ref, halo, level_cols in levels.values():
        width = level_cols + 2 * halo
        for r in range(halo):
            start = r * width + halo
            ref[side, start : start + level_cols] = recv(at, level_cols)
            at += level_cols
    corner = (2, 0, 4, 1) if side == 0 else (0, 4, 1, 2)
    for edge in range(2):
        for level in corner:
            ref, halo, level_cols = levels[level]
            width = level_cols + 2 * halo
            for r in range(halo):
                start = r * width + (0 if edge == 0 else halo + level_cols)
                ref[side, start : start + halo] = recv(at, halo)
                at += halo


def contract(lhs, count, tables, chunk=4):
    total = None
    for start in range(0, len(tables), chunk):
        group = tables[start : start + chunk]
        block = lhs[0:count, :, start * WIDE : (start + len(group)) * WIDE]
        weights = jnp.concatenate([read() for read in group], 0)
        part = dot(block.reshape(count * PAIRS, len(group) * WIDE), weights)
        total = part if total is None else total + part
    return total


def masked(tiles, words, bit):
    parts = []
    for n, (i, j) in enumerate(words[1]):
        kept = jnp.bitwise_and(words[0][i, j : j + 1, :], jnp.int32(1 << bit)) != 0
        kept = jnp.broadcast_to(kept, (PAIRS, WIDE))
        parts.append(jnp.where(kept, tiles[n], jnp.zeros((), BF16)))
    return jnp.concatenate(parts, 0)


def windows_dot(entries, words, table):
    total = None
    for start in range(0, len(entries), 2):
        group = entries[start : start + 2]
        blocks = [masked(read(), words, bit) for bit, read, _ in group]
        weights = [table[at] for _, _, at in group]
        part = dot(jnp.concatenate(blocks, 1), jnp.concatenate(weights, 0))
        total = part if total is None else total + part
    return total


def far_slots(level, row_par, col_par):
    return [
        (bit, a, b, 49 * level + offset_index((a, b), row_par, col_par))
        for bit, (a, b) in enumerate(window_slots(row_par, col_par))
    ]


def own_far(level, words, padded, table, out):
    half_rows, half_cols = words.shape[0] // 2, words.shape[1] // 2
    grid = padded.reshape(half_rows + 2, 2, half_cols + 2, 2, PAIRS, WIDE)
    for c, (row_par, col_par) in enumerate(CLASSES):
        spots = [
            (2 * i + row_par, 2 * j + col_par) for i in range(half_rows) for j in range(half_cols)
        ]

        def read(a, b):
            value = grid[a // 2 : a // 2 + half_rows, a % 2, b // 2 : b // 2 + half_cols, b % 2]
            return value.reshape(half_rows * half_cols, PAIRS, WIDE)

        entries = [
            (bit, functools.partial(read, a, b), at)
            for bit, a, b, at in far_slots(level, row_par, col_par)
        ]
        total = windows_dot(entries, (words, spots), table)
        out[c] = total.reshape(half_rows, half_cols * PAIRS, WIDE)


def own_kernel(row_tiles, *refs):
    (
        words_near, words0, words1, words2, field, q0, q1, q2, recv_l, recv_r, table,
        near, c0, c1, c2, p0, p1, p2, pf,
    ) = refs
    rows, cols = field.shape[0], field.shape[1]
    fill_windows((q0, q1, q2, field), recv_l, recv_r, (p0, p1, p2, pf))
    own_far(0, words0, p0, table, c0)
    own_far(1, words1, p1, table, c1)
    own_far(2, words2, p2, table, c2)
    grid = pf.reshape(rows + 2, cols + 2, PAIRS, WIDE)
    for top in range(0, rows, row_tiles):

        def read(u, v):
            value = grid[top + u : top + u + row_tiles, v : v + cols]
            return value.reshape(row_tiles * cols, PAIRS, WIDE)

        spots = [(top + i, j) for i in range(row_tiles) for j in range(cols)]
        entries = [
            (3 * u + v, functools.partial(read, u, v), NEAR_AT + 3 * u + v)
            for u in range(3)
            for v in range(3)
        ]
        total = windows_dot(entries, (words_near, spots), table)
        near[top : top + row_tiles] = total.reshape(row_tiles, cols, PAIRS, WIDE)


def far_level(level, words, partial, edges, table, parent, out):
    half_rows, half_cols = out.shape[0] // 2, out.shape[1] // 2
    above = tiles_of(parent[...])
    for c, (row_par, col_par) in enumerate(CLASSES):
        down = dot(above, table[DOWN_AT + 4 * level + c])
        total = partial[c] + down.reshape(half_rows, half_cols * PAIRS, WIDE)
        for side in range(2):
            grid = edges.at[side].reshape(2, half_cols + 2, 2, PAIRS, WIDE)
            first = 4 * side
            i = side * (half_rows - 1)
            spots = [(2 * i + row_par, 2 * j + col_par) for j in range(half_cols)]

            def read(a, b):
                return grid[a, b // 2 : b // 2 + half_cols, b % 2]

            entries = [
                (bit, functools.partial(read, a - first, b), at)
                for bit, a, b, at in far_slots(level, row_par, col_par)
                if first <= a < first + 2
            ]
            added = windows_dot(entries, (words, spots), table)[None]
            if half_rows == 1:
                total = total + added
            elif side == 0:
                total = jnp.concatenate([total[:1] + added, total[1:]], 0)
            else:
                total = jnp.concatenate([total[:-1], total[-1:] + added], 0)
        halves(out)[:, row_par, :, col_par] = total.astype(BF16).reshape(
            half_rows, half_cols, PAIRS, WIDE
        )


def product_kernel(last, *refs):
    (
        place, mask_top, words_near, words0, words1, words2, near, c0, c1, c2, column,
        recv_in, recv_out, table, basis,
    ) = refs[:15]
    outs = refs[15 : 16 if last else 24]
    e0, e1, e2, p3, ef, g0, g1, g2, g3, near_edge, lhs = refs[16 if last else 24 :]
    rows, cols = near.shape[0], near.shape[1]
    count = column.shape[0]
    inner = place[2] * place[3] == 0

    def pick(first, second, at, size):
        return jnp.where(inner, first[at : at + size], second[at : at + size])

    edges = (e0, e1, e2, ef)
    fill_edges(cols, functools.partial(pick, recv_out, recv_in), edges, 0)
    fill_edges(cols, functools.partial(pick, recv_in, recv_out), edges, 1)
    p3[0:count] = column[...]
    p3[count] = jnp.zeros((PAIRS, WIDE), BF16)
    for j in range(2):
        reads = []
        for k in range(SLOTS):
            tile, at = top_entry(place, mask_top, j, k, count // 6)
            lhs[0, :, k * WIDE : (k + 1) * WIDE] = p3[tile]
            reads.append(functools.partial(lambda at: table[3 * 49 + at], at))
        g3[0, j] = contract(lhs, 1, reads).astype(BF16)
    far_level(2, words2, c2, e2, table, g3, g2)
    far_level(1, words1, c1, e1, table, g2, g1)
    far_level(0, words0, c0, e0, table, g1, g0)
    for side in range(2):
        spots = [(side * (rows - 1), j) for j in range(cols)]
        entries = [
            (
                6 * side + v,
                functools.partial(lambda v: ef[side, v : v + cols], v),
                NEAR_AT + 6 * side + v,
            )
            for v in range(3)
        ]
        total = windows_dot(entries, (words_near, spots), table)
        near_edge[side] = total.reshape(cols, PAIRS, WIDE)
    near_edge[2] = jnp.zeros((cols, PAIRS, WIDE), F32)
    result = outs[0]

    def leaf_rows(step, carry):
        for part in range(2):
            i = 2 * step + part
            edge = jnp.where(i == 0, 0, jnp.where(i == rows - 1, 1, 2))
            for j in range(cols):
                far = dot_t(g0[i, j], basis[i * cols + j])
                result[i, j] = (near[i, j] + near_edge[edge, j] + far).astype(BF16)
        return carry

    lax.fori_loop(0, rows // 2, leaf_rows, 0)
    if not last:
        upward_pass(result, basis, table, UP_AT, *outs[1:])


def half_lanes(rows):
    return lax.broadcasted_iota(jnp.int32, (rows, WIDE), 1) < WIDE // 2


def expand_pair(first, second, order):
    low = half_lanes(RANK // 2)
    one, two = first.astype(F32), second.astype(F32)
    upper = jnp.where(low, one, pltpu.roll(two, WIDE // 2, 1))
    lower = jnp.where(low, pltpu.roll(one, WIDE // 2, 1), two)
    both = dot(order, jnp.concatenate([upper, lower], 0).astype(BF16))
    turned = pltpu.roll(both, WIDE // 2, 1)
    low = half_lanes(RANK)
    zero = jnp.zeros((), F32)
    blocks = [
        (jnp.where(low, both, zero), jnp.where(low, zero, turned)),
        (jnp.where(low, turned, zero), jnp.where(low, zero, both)),
    ]
    return [jnp.concatenate(pair, 0) for pair in blocks]


def row_order():
    to = lax.broadcasted_iota(jnp.int32, (RANK, RANK), 0)
    source = lax.broadcasted_iota(jnp.int32, (RANK, RANK), 1)
    return (source == (to % 2) * (RANK // 2) + to // 2).astype(F32).astype(BF16)


def expand(packed, out, base, unroll):
    order = row_order()
    count = packed.shape[0]

    def pair(at, after):
        one, two = expand_pair(packed[at], packed[after], order)
        out[base + at] = one.astype(BF16)
        if after is not at:
            out[base + after] = two.astype(BF16)

    def some(n, carry):
        for k in range(unroll):
            at = 2 * (n * unroll + k)
            pair(at, at + 1)
        return carry

    steps = count // 2 // unroll
    lax.fori_loop(0, steps, some, 0)
    for at in range(2 * unroll * steps, count, 2):
        pair(at, at + 1 if at + 1 < count else at)


def mask_words(mask, out):
    slots = mask.shape[2]
    slot = lax.broadcasted_iota(jnp.int32, (slots, WIDE), 0)

    def powers(low, high):
        value = jnp.where((slot >= low) & (slot < high), jnp.left_shift(1, slot - low), 0)
        return value.astype(F32).astype(BF16)

    for i in range(mask.shape[0]):
        row = (mask[i] != 0).astype(F32).astype(BF16)
        word = dot(row, powers(0, min(14, slots))).astype(jnp.int32)
        if slots > 14:
            word = word + jnp.left_shift(dot(row, powers(14, slots)).astype(jnp.int32), 14)
        out[i] = word


def first_kernel(*refs):
    field, packed_basis, packed, packed_up, packed_near = refs[:5]
    masks, (basis, table), words, outs = refs[5:9], refs[9:11], refs[11:15], refs[15:]
    expand(packed_basis, basis, 0, 8)
    expand(packed_up, table, UP_AT, 6)
    expand(packed, table, 0, 7)
    expand(packed_near, table, NEAR_AT, 4)
    for k in range(12):
        wide = table[UP_AT + k].astype(F32)
        table[DOWN_AT + k] = jnp.swapaxes(wide, 0, 1).astype(BF16)
    for mask, out in zip(masks, words):
        mask_words(mask, out)
    upward_pass(field, basis, table, UP_AT, *outs)


def shape_of(*dims):
    return jax.ShapeDtypeStruct(tuple(dims) + (PAIRS, WIDE), BF16)


def upward_shapes(rows, cols):
    counts, _, _ = message_sizes(rows)
    edge = 2 * cols + cols + cols + cols // 2
    return [
        shape_of(rows, cols),
        shape_of(rows // 2, cols // 2),
        shape_of(rows // 4, cols // 4),
        shape_of(rows // 8, cols // 8),
        shape_of(sum(counts)),
        shape_of(sum(counts)),
        shape_of(edge),
        shape_of(edge),
    ]


VMEM = pl.BlockSpec(memory_space=pltpu.VMEM)
SMEM = pl.BlockSpec(memory_space=pltpu.SMEM)


PARAMS = pltpu.CompilerParams(vmem_limit_bytes=24 * 1024 * 1024)


def start_up(field, packed, masks):
    rows, cols = field.shape[0], field.shape[1]
    outs = [jax.ShapeDtypeStruct((rows * cols, WIDE, WIDE), BF16)]
    outs += [jax.ShapeDtypeStruct((DOWN_AT + 12, WIDE, WIDE), BF16)]
    outs += [jax.ShapeDtypeStruct(mask.shape[:2] + (WIDE,), jnp.int32) for mask in masks]
    outs += upward_shapes(rows, cols)
    return pl.pallas_call(
        first_kernel,
        out_shape=outs,
        in_specs=[VMEM] * 9,
        out_specs=[VMEM] * len(outs),
        compiler_params=PARAMS,
    )(field, *packed, *masks)


def tile_scratch(*dims):
    return pltpu.VMEM(tuple(dims) + (PAIRS, WIDE), BF16)


def far_shape(rows, cols):
    return jax.ShapeDtypeStruct((4, rows // 2, cols // 2 * PAIRS, WIDE), F32)


def own_part(words, field, q0, q1, q2, recv_l, recv_r, table):
    rows, cols = field.shape[0], field.shape[1]
    outs = [
        jax.ShapeDtypeStruct((rows, cols, PAIRS, WIDE), F32),
        far_shape(rows, cols),
        far_shape(rows // 2, cols // 2),
        far_shape(rows // 4, cols // 4),
    ]
    args = (*words, field, q0, q1, q2, recv_l, recv_r, table)
    return pl.pallas_call(
        functools.partial(own_kernel, 2),
        out_shape=outs,
        in_specs=[VMEM] * len(args),
        out_specs=[VMEM] * len(outs),
        scratch_shapes=[
            tile_scratch((rows + 4) * (cols + 4)),
            tile_scratch((rows // 2 + 4) * (cols // 2 + 4)),
            tile_scratch((rows // 4 + 4) * (cols // 4 + 4)),
            tile_scratch((rows + 2) * (cols + 2)),
        ],
        compiler_params=PARAMS,
        cost_estimate=pl.CostEstimate(
            flops=7 * 10**9, bytes_accessed=16 * 10**6, transcendentals=0
        ),
    )(*args)


def product(last, place, mask_top, words, own, column, received, table, basis):
    rows, cols = own[0].shape[0], own[0].shape[1]
    outs = [shape_of(rows, cols)]
    if not last:
        outs += upward_shapes(rows, cols)
    args = (place, mask_top, *words, *own, column, *received, table, basis)
    return pl.pallas_call(
        functools.partial(product_kernel, last),
        out_shape=outs,
        in_specs=[SMEM] * 2 + [VMEM] * (len(args) - 2),
        out_specs=[VMEM] * len(outs),
        scratch_shapes=[
            tile_scratch(2, 2 * (cols + 4)),
            tile_scratch(2, 2 * (cols // 2 + 4)),
            tile_scratch(2, 2 * (cols // 4 + 4)),
            tile_scratch(column.shape[0] + 1),
            tile_scratch(2, cols + 2),
            tile_scratch(rows, cols),
            tile_scratch(rows // 2, cols // 2),
            tile_scratch(rows // 4, cols // 4),
            tile_scratch(rows // 8, cols // 8),
            pltpu.VMEM((3, cols, PAIRS, WIDE), F32),
            pltpu.VMEM((1, PAIRS, SLOTS * WIDE), BF16),
        ],
        compiler_params=PARAMS,
        cost_estimate=pl.CostEstimate(
            flops=8 * 10**9, bytes_accessed=16 * 10**6, transcendentals=0
        ),
    )(*args)


def shift(value, axis, step):
    count = lax.axis_size(axis)
    pairs = [(i, i + step) for i in range(count) if 0 <= i + step < count]
    return lax.ppermute(value, axis, pairs)


def two_by_two():
    return lax.axis_size("rhs") == 2 and lax.axis_size("sub") == 2


def exchange_cols(send_l, send_r):
    return shift(send_r, "br", 1), shift(send_l, "br", -1)


def exchange_rows(rows, q3, recv_l, recv_r, send_u, send_d, own):
    counts, up, down = message_sizes(rows)
    last = down[1]
    wide = jnp.concatenate([q3[0], recv_l[last:], recv_r[last:]], 0)
    tail = []
    swap = [(0, 1), (1, 0)]
    if two_by_two():
        tail = [wide, lax.ppermute(wide, "sub", swap)]
    up_message = jnp.concatenate([send_u, recv_l[up[0] : up[1]], recv_r[up[0] : up[1]], *tail], 0)
    down_message = jnp.concatenate(
        [send_d, recv_l[down[0] : down[1]], recv_r[down[0] : down[1]], *tail], 0
    )
    if two_by_two():
        outer = lax.axis_index("sub") == 1
        across = jnp.where(outer, down_message, up_message)
        within = jnp.where(outer, up_message, down_message)
        recv_out = lax.ppermute(across, ROW_AXES, [(1, 2), (2, 1)])
        recv_in = lax.ppermute(within, "sub", swap)
        recv_out, *own = lax.optimization_barrier((recv_out, *own))
        mine = recv_out[up_message.shape[0] - 2 * wide.shape[0] :]
        far = mine + lax.ppermute(mine, "sub", swap)
        column = jnp.concatenate([*tail, far], 0)
    else:
        recv_in = shift(up_message, ROW_AXES, -1)
        recv_out = shift(down_message, ROW_AXES, 1)
        column = lax.all_gather(wide, ROW_AXES, axis=0, tiled=True)
    return column, (recv_in, recv_out), own


def on_device(
    sources, leaf_basis, transfer, coupling, near_table, near_mask,
    mask_leaf, mask_mid, mask_upper, mask_top,
):
    rows, cols = sources.shape[0], sources.shape[1]
    row = lax.axis_index(ROW_AXES)
    field = sources.reshape(rows, cols, PAIRS, WIDE)
    packed = (
        leaf_basis.reshape(rows * cols, LEAF // 2, WIDE),
        coupling.reshape(4 * 49, RANK // 2, WIDE),
        transfer.reshape(12, RANK // 2, WIDE),
        near_table.reshape(9, LEAF // 2, WIDE),
    )
    upper = lax.dynamic_slice_in_dim(mask_upper, row * (rows // 4), rows // 4, 0)
    basis, table, *rest = start_up(field, packed, (near_mask, mask_leaf, mask_mid, upper))
    words, (q0, q1, q2, q3), sends = rest[:4], rest[4:8], rest[8:]
    folded = 1 if two_by_two() else 0
    place = jnp.stack([row, lax.axis_index("rhs"), lax.axis_index("sub"), jnp.int32(folded)])
    for step in range(PRODUCTS):
        send_l, send_r, send_u, send_d = sends
        recv_l, recv_r = exchange_cols(send_l, send_r)
        own = own_part(words, field, q0, q1, q2, recv_l, recv_r, table)
        column, received, own = exchange_rows(rows, q3, recv_l, recv_r, send_u, send_d, own)
        last = step == PRODUCTS - 1
        outs = product(last, place, mask_top, words, own, column, received, table, basis)
        field = outs[0]
        if not last:
            q0, q1, q2, q3, *sends = outs[1:]
    return field.reshape(rows, cols, SIDES * LEAF)


def solution(mesh):
    placed = (
        P(("grp", "rhs", "sub"), "br", None),
        P(("grp", "rhs", "sub"), "br", None),
        P(),
        P(),
        P(),
        P(("grp", "rhs", "sub"), "br", None),
        P(("grp", "rhs", "sub"), "br", None),
        P(("grp", "rhs", "sub"), "br", None),
        P("grp", "br", None),
        P("grp", "br", None),
    )
    return jax.shard_map(
        on_device,
        mesh=mesh,
        in_specs=placed,
        out_specs=P(("grp", "rhs", "sub"), "br", None),
        check_vma=False,
    )
```

```python
import functools

import jax
import jax.numpy as jnp
from jax import lax
from jax.experimental import pallas as pl
from jax.experimental.pallas import tpu as pltpu
from jax.sharding import PartitionSpec as P

LEAF = 64
RANK = 64
SIDES = 32
PRODUCTS = 3
PAIRS = SIDES // 2
WIDE = 2 * RANK
SLOTS = 27
ROW_AXES = ("rhs", "sub")
UP_AT = 4 * 49
NEAR_AT = UP_AT + 12
DOWN_AT = NEAR_AT + 9
BF16 = jnp.bfloat16
F32 = jnp.float32


def window_slots(row_par, col_par):
    slots = []
    for a in range(6):
        for b in range(6):
            if abs(a - 2 - row_par) <= 1 and abs(b - 2 - col_par) <= 1:
                continue
            slots.append((a, b))
    return slots


def offset_index(slot, row_par, col_par):
    return 7 * (slot[0] + 1 - row_par) + slot[1] + 1 - col_par


CLASSES = [(row_par, col_par) for row_par in range(2) for col_par in range(2)]


def top_entry(place, mask, col_par, k, count):
    row, rhs, sub, folded = place[0], place[1], place[2], place[3]
    parity = jnp.bitwise_and(row, 1)
    even, odd = [window_slots(row_par, col_par)[k] for row_par in range(2)]
    spots = [2, 3, 0, 1, 4, 5]

    def pick(first, second):
        return jnp.where(parity == 0, jnp.int32(first), jnp.int32(second))

    source = row - parity + pick(even[0], odd[0]) - 2
    inner = jnp.bitwise_and(source, 1)
    near_place = jnp.where(inner == sub, 0, 1)
    far_place = jnp.where(inner == rhs, 2, 3)
    two = jnp.where(jnp.right_shift(source, 1) == rhs, near_place, far_place)
    at = jnp.where(folded == 1, two, source)
    kept = (mask[row, col_par, k] != 0) & (source >= 0) & (source < count)
    tile = jnp.where(kept, at * 6 + pick(spots[even[1]], spots[odd[1]]), 6 * count)
    return tile, pick(offset_index(even, 0, col_par), offset_index(odd, 1, col_par))


def dot(a, b):
    return jnp.dot(a, b, preferred_element_type=F32)


def dot_t(a, b):
    return lax.dot_general(a, b, (((1,), (1,)), ((), ())), preferred_element_type=F32)


def halves(ref):
    rows, cols = ref.shape[0], ref.shape[1]
    return ref.reshape(rows // 2, 2, cols // 2, 2, PAIRS, WIDE)


def tiles_of(value):
    return value.reshape(-1, WIDE)


def climb(child, parent, table, first):
    rows, cols = parent.shape[0], parent.shape[1]
    total = None
    for c, (a, b) in enumerate(CLASSES):
        block = tiles_of(halves(child)[:, a, :, b])
        part = dot(block, table[first + c])
        total = part if total is None else total + part
    parent[...] = total.astype(BF16).reshape(rows, cols, PAIRS, WIDE)


def upward_pass(field, basis, table, first, q0, q1, q2, q3, send_l, send_r, send_u, send_d):
    rows, cols = field.shape[0], field.shape[1]

    def leaf_rows(step, carry):
        for part in range(2):
            i = 2 * step + part
            for j in range(cols):
                q0[i, j] = dot(field[i, j], basis[i * cols + j]).astype(BF16)
        return carry

    lax.fori_loop(0, rows // 2, leaf_rows, 0)
    climb(q0, q1, table, first + 0)
    climb(q1, q2, table, first + 4)
    climb(q2, q3, table, first + 8)
    for ref, side in ((send_l, 0), (send_r, 1)):
        at = 0
        for source, first, last, width in col_message(rows):
            level = (q0, q1, q2, q3, field)[source]
            low = 0 if side == 0 else level.shape[1] - width
            for r in range(first, last):
                ref[at : at + width] = level[r, low : low + width]
                at += width
    for ref, side in ((send_u, 0), (send_d, 1)):
        at = 0
        for level, width in ((q0, 2), (field, 1), (q1, 2), (q2, 2)):
            low = 0 if side == 0 else level.shape[0] - width
            for r in range(low, low + width):
                ref[at : at + level.shape[1]] = level[r]
                at += level.shape[1]


def col_message(rows):
    return [
        (0, 2, rows - 2, 2),
        (4, 1, rows - 1, 1),
        (0, 0, 2, 2),
        (4, 0, 1, 1),
        (1, 0, 2, 2),
        (2, 0, rows // 4, 2),
        (0, rows - 2, rows, 2),
        (4, rows - 1, rows, 1),
        (1, rows // 2 - 2, rows // 2, 2),
        (3, 0, rows // 8, 2),
    ]


def message_sizes(rows):
    counts = [(last - first) * width for _, first, last, width in col_message(rows)]
    start = sum(counts[:2])
    up = (start, start + sum(counts[2:6]))
    down = (start + sum(counts[2:5]), start + sum(counts[2:9]))
    return counts, up, down


def fill_windows(own, recv_l, recv_r, pads):
    q0, q1, q2, field = own
    p0, p1, p2, pf = pads
    rows = q0.shape[0]
    levels = {0: (p0, 2, q0), 1: (p1, 2, q1), 2: (p2, 2, q2), 4: (pf, 1, field)}
    for ref, halo, source in levels.values():
        level_rows, level_cols = source.shape[0], source.shape[1]
        width = level_cols + 2 * halo
        blank = jnp.zeros((halo * width, PAIRS, WIDE), BF16)
        ref[0 : halo * width] = blank
        ref[(halo + level_rows) * width : (2 * halo + level_rows) * width] = blank
        for r in range(level_rows):
            start = (r + halo) * width + halo
            ref[start : start + level_cols] = source[r]
    for recv, side in ((recv_l, 0), (recv_r, 1)):
        at = 0
        for level, first, last, count in col_message(rows)[:-1]:
            ref, halo, source = levels[level]
            level_cols = source.shape[1]
            width = level_cols + 2 * halo
            for r in range(first, last):
                start = (r + halo) * width + (0 if side == 0 else halo + level_cols)
                ref[start : start + count] = recv[at : at + count]
                at += count


def fill_edges(cols, recv, pads, side):
    p0, p1, p2, pf = pads
    levels = {0: (p0, 2, cols), 4: (pf, 1, cols), 1: (p1, 2, cols // 2), 2: (p2, 2, cols // 4)}
    at = 0
    for ref, halo, level_cols in levels.values():
        width = level_cols + 2 * halo
        for r in range(halo):
            start = r * width + halo
            ref[side, start : start + level_cols] = recv(at, level_cols)
            at += level_cols
    corner = (2, 0, 4, 1) if side == 0 else (0, 4, 1, 2)
    for edge in range(2):
        for level in corner:
            ref, halo, level_cols = levels[level]
            width = level_cols + 2 * halo
            for r in range(halo):
                start = r * width + (0 if edge == 0 else halo + level_cols)
                ref[side, start : start + halo] = recv(at, halo)
                at += halo


def contract(lhs, count, tables, chunk=4):
    total = None
    for start in range(0, len(tables), chunk):
        group = tables[start : start + chunk]
        block = lhs[0:count, :, start * WIDE : (start + len(group)) * WIDE]
        weights = jnp.concatenate([read() for read in group], 0)
        part = dot(block.reshape(count * PAIRS, len(group) * WIDE), weights)
        total = part if total is None else total + part
    return total


def masked(tiles, words, bit):
    parts = []
    for n, (i, j) in enumerate(words[1]):
        kept = jnp.bitwise_and(words[0][i, j : j + 1, :], jnp.int32(1 << bit)) != 0
        kept = jnp.broadcast_to(kept, (PAIRS, WIDE))
        parts.append(jnp.where(kept, tiles[n], jnp.zeros((), BF16)))
    return jnp.concatenate(parts, 0)


def windows_dot(entries, words, table):
    total = None
    for start in range(0, len(entries), 2):
        group = entries[start : start + 2]
        blocks = [masked(read(), words, bit) for bit, read, _ in group]
        weights = [table[at] for _, _, at in group]
        part = dot(jnp.concatenate(blocks, 1), jnp.concatenate(weights, 0))
        total = part if total is None else total + part
    return total


def far_slots(level, row_par, col_par):
    return [
        (bit, a, b, 49 * level + offset_index((a, b), row_par, col_par))
        for bit, (a, b) in enumerate(window_slots(row_par, col_par))
    ]


def own_far(level, words, padded, table, out):
    half_rows, half_cols = words.shape[0] // 2, words.shape[1] // 2
    grid = padded.reshape(half_rows + 2, 2, half_cols + 2, 2, PAIRS, WIDE)
    for c, (row_par, col_par) in enumerate(CLASSES):
        spots = [
            (2 * i + row_par, 2 * j + col_par) for i in range(half_rows) for j in range(half_cols)
        ]

        def read(a, b):
            value = grid[a // 2 : a // 2 + half_rows, a % 2, b // 2 : b // 2 + half_cols, b % 2]
            return value.reshape(half_rows * half_cols, PAIRS, WIDE)

        entries = [
            (bit, functools.partial(read, a, b), at)
            for bit, a, b, at in far_slots(level, row_par, col_par)
        ]
        total = windows_dot(entries, (words, spots), table)
        out[c] = total.reshape(half_rows, half_cols * PAIRS, WIDE)


def own_kernel(row_tiles, *refs):
    (
        words_near, words0, words1, words2, field, q0, q1, q2, recv_l, recv_r, table,
        near, c0, c1, c2, p0, p1, p2, pf,
    ) = refs
    rows, cols = field.shape[0], field.shape[1]
    fill_windows((q0, q1, q2, field), recv_l, recv_r, (p0, p1, p2, pf))
    own_far(0, words0, p0, table, c0)
    own_far(1, words1, p1, table, c1)
    own_far(2, words2, p2, table, c2)
    grid = pf.reshape(rows + 2, cols + 2, PAIRS, WIDE)
    for top in range(0, rows, row_tiles):

        def read(u, v):
            value = grid[top + u : top + u + row_tiles, v : v + cols]
            return value.reshape(row_tiles * cols, PAIRS, WIDE)

        spots = [(top + i, j) for i in range(row_tiles) for j in range(cols)]
        entries = [
            (3 * u + v, functools.partial(read, u, v), NEAR_AT + 3 * u + v)
            for u in range(3)
            for v in range(3)
        ]
        total = windows_dot(entries, (words_near, spots), table)
        near[top : top + row_tiles] = total.reshape(row_tiles, cols, PAIRS, WIDE)


def far_level(level, words, partial, edges, table, parent, out):
    half_rows, half_cols = out.shape[0] // 2, out.shape[1] // 2
    above = tiles_of(parent[...])
    for c, (row_par, col_par) in enumerate(CLASSES):
        down = dot(above, table[DOWN_AT + 4 * level + c])
        total = partial[c] + down.reshape(half_rows, half_cols * PAIRS, WIDE)
        for side in range(2):
            grid = edges.at[side].reshape(2, half_cols + 2, 2, PAIRS, WIDE)
            first = 4 * side
            i = side * (half_rows - 1)
            spots = [(2 * i + row_par, 2 * j + col_par) for j in range(half_cols)]

            def read(a, b):
                return grid[a, b // 2 : b // 2 + half_cols, b % 2]

            entries = [
                (bit, functools.partial(read, a - first, b), at)
                for bit, a, b, at in far_slots(level, row_par, col_par)
                if first <= a < first + 2
            ]
            added = windows_dot(entries, (words, spots), table)[None]
            if half_rows == 1:
                total = total + added
            elif side == 0:
                total = jnp.concatenate([total[:1] + added, total[1:]], 0)
            else:
                total = jnp.concatenate([total[:-1], total[-1:] + added], 0)
        halves(out)[:, row_par, :, col_par] = total.astype(BF16).reshape(
            half_rows, half_cols, PAIRS, WIDE
        )


def product_kernel(last, *refs):
    (
        place, mask_top, words_near, words0, words1, words2, near, c0, c1, c2, column,
        recv_in, recv_out, table, basis,
    ) = refs[:15]
    outs = refs[15 : 16 if last else 24]
    e0, e1, e2, p3, ef, g0, g1, g2, g3, near_edge, lhs = refs[16 if last else 24 :]
    rows, cols = near.shape[0], near.shape[1]
    count = column.shape[0]
    inner = place[2] * place[3] == 0

    def pick(first, second, at, size):
        return jnp.where(inner, first[at : at + size], second[at : at + size])

    edges = (e0, e1, e2, ef)
    fill_edges(cols, functools.partial(pick, recv_out, recv_in), edges, 0)
    fill_edges(cols, functools.partial(pick, recv_in, recv_out), edges, 1)
    p3[0:count] = column[...]
    p3[count] = jnp.zeros((PAIRS, WIDE), BF16)
    for j in range(2):
        reads = []
        for k in range(SLOTS):
            tile, at = top_entry(place, mask_top, j, k, count // 6)
            lhs[0, :, k * WIDE : (k + 1) * WIDE] = p3[tile]
            reads.append(functools.partial(lambda at: table[3 * 49 + at], at))
        g3[0, j] = contract(lhs, 1, reads).astype(BF16)
    far_level(2, words2, c2, e2, table, g3, g2)
    far_level(1, words1, c1, e1, table, g2, g1)
    far_level(0, words0, c0, e0, table, g1, g0)
    for side in range(2):
        spots = [(side * (rows - 1), j) for j in range(cols)]
        entries = [
            (
                6 * side + v,
                functools.partial(lambda v: ef[side, v : v + cols], v),
                NEAR_AT + 6 * side + v,
            )
            for v in range(3)
        ]
        total = windows_dot(entries, (words_near, spots), table)
        near_edge[side] = total.reshape(cols, PAIRS, WIDE)
    near_edge[2] = jnp.zeros((cols, PAIRS, WIDE), F32)
    result = outs[0]

    def leaf_rows(step, carry):
        for part in range(2):
            i = 2 * step + part
            edge = jnp.where(i == 0, 0, jnp.where(i == rows - 1, 1, 2))
            for j in range(cols):
                far = dot_t(g0[i, j], basis[i * cols + j])
                result[i, j] = (near[i, j] + near_edge[edge, j] + far).astype(BF16)
        return carry

    lax.fori_loop(0, rows // 2, leaf_rows, 0)
    if not last:
        upward_pass(result, basis, table, UP_AT, *outs[1:])


def half_lanes(rows):
    return lax.broadcasted_iota(jnp.int32, (rows, WIDE), 1) < WIDE // 2


def expand_pair(first, second, order):
    low = half_lanes(RANK // 2)
    one, two = first.astype(F32), second.astype(F32)
    upper = jnp.where(low, one, pltpu.roll(two, WIDE // 2, 1))
    lower = jnp.where(low, pltpu.roll(one, WIDE // 2, 1), two)
    both = dot(order, jnp.concatenate([upper, lower], 0).astype(BF16))
    turned = pltpu.roll(both, WIDE // 2, 1)
    low = half_lanes(RANK)
    zero = jnp.zeros((), F32)
    blocks = [
        (jnp.where(low, both, zero), jnp.where(low, zero, turned)),
        (jnp.where(low, turned, zero), jnp.where(low, zero, both)),
    ]
    return [jnp.concatenate(pair, 0) for pair in blocks]


def row_order():
    to = lax.broadcasted_iota(jnp.int32, (RANK, RANK), 0)
    source = lax.broadcasted_iota(jnp.int32, (RANK, RANK), 1)
    return (source == (to % 2) * (RANK // 2) + to // 2).astype(F32).astype(BF16)


def expand(packed, out, base, unroll):
    order = row_order()
    count = packed.shape[0]

    def pair(at, after):
        one, two = expand_pair(packed[at], packed[after], order)
        out[base + at] = one.astype(BF16)
        if after is not at:
            out[base + after] = two.astype(BF16)

    def some(n, carry):
        for k in range(unroll):
            at = 2 * (n * unroll + k)
            pair(at, at + 1)
        return carry

    steps = count // 2 // unroll
    lax.fori_loop(0, steps, some, 0)
    for at in range(2 * unroll * steps, count, 2):
        pair(at, at + 1 if at + 1 < count else at)


def first_kernel(field, packed_basis, packed_up, basis, *rest):
    outs, up_table = rest[:-1], rest[-1]
    expand(packed_basis, basis, 0, 8)
    expand(packed_up, up_table, 0, 6)
    upward_pass(field, basis, up_table, 0, *outs)


def mask_words(mask, out):
    slots = mask.shape[2]
    slot = lax.broadcasted_iota(jnp.int32, (slots, WIDE), 0)

    def powers(low, high):
        value = jnp.where((slot >= low) & (slot < high), jnp.left_shift(1, slot - low), 0)
        return value.astype(F32).astype(BF16)

    for i in range(mask.shape[0]):
        row = (mask[i] != 0).astype(F32).astype(BF16)
        word = dot(row, powers(0, min(14, slots))).astype(jnp.int32)
        if slots > 14:
            word = word + jnp.left_shift(dot(row, powers(14, slots)).astype(jnp.int32), 14)
        out[i] = word


def table_kernel(packed, packed_up, packed_near, near_mask, mask0, mask1, mask2, table, *words):
    expand(packed, table, 0, 7)
    expand(packed_up, table, UP_AT, 6)
    expand(packed_near, table, NEAR_AT, 4)
    for k in range(12):
        wide = table[UP_AT + k].astype(F32)
        table[DOWN_AT + k] = jnp.swapaxes(wide, 0, 1).astype(BF16)
    for mask, out in zip((near_mask, mask0, mask1, mask2), words):
        mask_words(mask, out)


def shape_of(*dims):
    return jax.ShapeDtypeStruct(tuple(dims) + (PAIRS, WIDE), BF16)


def upward_shapes(rows, cols):
    counts, _, _ = message_sizes(rows)
    edge = 2 * cols + cols + cols + cols // 2
    return [
        shape_of(rows, cols),
        shape_of(rows // 2, cols // 2),
        shape_of(rows // 4, cols // 4),
        shape_of(rows // 8, cols // 8),
        shape_of(sum(counts)),
        shape_of(sum(counts)),
        shape_of(edge),
        shape_of(edge),
    ]


VMEM = pl.BlockSpec(memory_space=pltpu.VMEM)
SMEM = pl.BlockSpec(memory_space=pltpu.SMEM)


def grant(size):
    return pltpu.CompilerParams(vmem_limit_bytes=size * 1024 * 1024)


def start_up(field, packed_basis, packed_up):
    rows, cols = field.shape[0], field.shape[1]
    outs = [jax.ShapeDtypeStruct((rows * cols, WIDE, WIDE), BF16)]
    outs += upward_shapes(rows, cols)
    return pl.pallas_call(
        first_kernel,
        out_shape=outs,
        in_specs=[VMEM] * 3,
        out_specs=[VMEM] * len(outs),
        scratch_shapes=[pltpu.VMEM((12, WIDE, WIDE), BF16)],
        compiler_params=grant(12),
    )(field, packed_basis, packed_up)


def build_tables(packed, masks):
    outs = [jax.ShapeDtypeStruct((DOWN_AT + 12, WIDE, WIDE), BF16)]
    outs += [jax.ShapeDtypeStruct(mask.shape[:2] + (WIDE,), jnp.int32) for mask in masks]
    return pl.pallas_call(
        table_kernel,
        out_shape=outs,
        in_specs=[VMEM] * 7,
        out_specs=[VMEM] * 5,
        compiler_params=grant(14),
        cost_estimate=pl.CostEstimate(
            flops=4 * 10**9, bytes_accessed=16 * 10**6, transcendentals=0
        ),
    )(*packed, *masks)


def tile_scratch(*dims):
    return pltpu.VMEM(tuple(dims) + (PAIRS, WIDE), BF16)


def far_shape(rows, cols):
    return jax.ShapeDtypeStruct((4, rows // 2, cols // 2 * PAIRS, WIDE), F32)


def own_part(words, field, q0, q1, q2, recv_l, recv_r, table):
    rows, cols = field.shape[0], field.shape[1]
    outs = [
        jax.ShapeDtypeStruct((rows, cols, PAIRS, WIDE), F32),
        far_shape(rows, cols),
        far_shape(rows // 2, cols // 2),
        far_shape(rows // 4, cols // 4),
    ]
    args = (*words, field, q0, q1, q2, recv_l, recv_r, table)
    return pl.pallas_call(
        functools.partial(own_kernel, 2),
        out_shape=outs,
        in_specs=[VMEM] * len(args),
        out_specs=[VMEM] * len(outs),
        scratch_shapes=[
            tile_scratch((rows + 4) * (cols + 4)),
            tile_scratch((rows // 2 + 4) * (cols // 2 + 4)),
            tile_scratch((rows // 4 + 4) * (cols // 4 + 4)),
            tile_scratch((rows + 2) * (cols + 2)),
        ],
        compiler_params=grant(20),
    )(*args)


def product(last, place, mask_top, words, own, column, received, table, basis):
    rows, cols = own[0].shape[0], own[0].shape[1]
    outs = [shape_of(rows, cols)]
    if not last:
        outs += upward_shapes(rows, cols)
    args = (place, mask_top, *words, *own, column, *received, table, basis)
    return pl.pallas_call(
        functools.partial(product_kernel, last),
        out_shape=outs,
        in_specs=[SMEM] * 2 + [VMEM] * (len(args) - 2),
        out_specs=[VMEM] * len(outs),
        scratch_shapes=[
            tile_scratch(2, 2 * (cols + 4)),
            tile_scratch(2, 2 * (cols // 2 + 4)),
            tile_scratch(2, 2 * (cols // 4 + 4)),
            tile_scratch(column.shape[0] + 1),
            tile_scratch(2, cols + 2),
            tile_scratch(rows, cols),
            tile_scratch(rows // 2, cols // 2),
            tile_scratch(rows // 4, cols // 4),
            tile_scratch(rows // 8, cols // 8),
            pltpu.VMEM((3, cols, PAIRS, WIDE), F32),
            pltpu.VMEM((1, PAIRS, SLOTS * WIDE), BF16),
        ],
        compiler_params=grant(22),
        cost_estimate=pl.CostEstimate(
            flops=8 * 10**9, bytes_accessed=16 * 10**6, transcendentals=0
        ),
    )(*args)


def shift(value, axis, step):
    count = lax.axis_size(axis)
    pairs = [(i, i + step) for i in range(count) if 0 <= i + step < count]
    return lax.ppermute(value, axis, pairs)


def two_by_two():
    return lax.axis_size("rhs") == 2 and lax.axis_size("sub") == 2


def exchange_cols(send_l, send_r):
    return shift(send_r, "br", 1), shift(send_l, "br", -1)


def exchange_rows(rows, q3, recv_l, recv_r, send_u, send_d, packed, own_of):
    counts, up, down = message_sizes(rows)
    last = down[1]
    wide = jnp.concatenate([q3[0], recv_l[last:], recv_r[last:]], 0)
    tail = []
    swap = [(0, 1), (1, 0)]
    if two_by_two():
        tail = [wide, lax.ppermute(wide, "sub", swap)]
    up_message = jnp.concatenate([send_u, recv_l[up[0] : up[1]], recv_r[up[0] : up[1]], *tail], 0)
    down_message = jnp.concatenate(
        [send_d, recv_l[down[0] : down[1]], recv_r[down[0] : down[1]], *tail], 0
    )
    if two_by_two():
        outer = lax.axis_index("sub") == 1
        across = jnp.where(outer, down_message, up_message)
        within = jnp.where(outer, up_message, down_message)
        across, within, *packed = lax.optimization_barrier((across, within, *packed))
        recv_out = lax.ppermute(across, ROW_AXES, [(1, 2), (2, 1)])
        recv_in = lax.ppermute(within, "sub", swap)
        made, own = own_of(packed)
        recv_out, *own = lax.optimization_barrier((recv_out, *own))
        mine = recv_out[up_message.shape[0] - 2 * wide.shape[0] :]
        far = mine + lax.ppermute(mine, "sub", swap)
        column = jnp.concatenate([*tail, far], 0)
    else:
        recv_in = shift(up_message, ROW_AXES, -1)
        recv_out = shift(down_message, ROW_AXES, 1)
        column = lax.all_gather(wide, ROW_AXES, axis=0, tiled=True)
        made, own = own_of(packed)
    return column, (recv_in, recv_out), made, own


def on_device(
    sources, leaf_basis, transfer, coupling, near_table, near_mask,
    mask_leaf, mask_mid, mask_upper, mask_top,
):
    rows, cols = sources.shape[0], sources.shape[1]
    row = lax.axis_index(ROW_AXES)
    field = sources.reshape(rows, cols, PAIRS, WIDE)
    packed_basis = leaf_basis.reshape(rows * cols, LEAF // 2, WIDE)
    packed_up = transfer.reshape(12, RANK // 2, WIDE)
    basis, q0, q1, q2, q3, *sends = start_up(field, packed_basis, packed_up)
    packed = (
        coupling.reshape(4 * 49, RANK // 2, WIDE),
        packed_up,
        near_table.reshape(9, LEAF // 2, WIDE),
    )
    upper = lax.dynamic_slice_in_dim(mask_upper, row * (rows // 4), rows // 4, 0)
    masks = (near_mask, mask_leaf, mask_mid, upper)
    table = words = None
    folded = 1 if two_by_two() else 0
    place = jnp.stack([row, lax.axis_index("rhs"), lax.axis_index("sub"), jnp.int32(folded)])
    for step in range(PRODUCTS):
        send_l, send_r, send_u, send_d = sends
        recv_l, recv_r = exchange_cols(send_l, send_r)

        def own_of(held):
            made = (table, words)
            if made[0] is None:
                first, *others = build_tables(held, masks)
                made = (first, others)
            return made, own_part(made[1], field, q0, q1, q2, recv_l, recv_r, made[0])

        held = packed if step == 0 else ()
        column, received, made, own = exchange_rows(
            rows, q3, recv_l, recv_r, send_u, send_d, held, own_of
        )
        table, words = made
        last = step == PRODUCTS - 1
        outs = product(last, place, mask_top, words, own, column, received, table, basis)
        field = outs[0]
        if not last:
            q0, q1, q2, q3, *sends = outs[1:]
    return field.reshape(rows, cols, SIDES * LEAF)


def solution(mesh):
    placed = (
        P(("grp", "rhs", "sub"), "br", None),
        P(("grp", "rhs", "sub"), "br", None),
        P(),
        P(),
        P(),
        P(("grp", "rhs", "sub"), "br", None),
        P(("grp", "rhs", "sub"), "br", None),
        P(("grp", "rhs", "sub"), "br", None),
        P("grp", "br", None),
        P("grp", "br", None),
    )
    return jax.shard_map(
        on_device,
        mesh=mesh,
        in_specs=placed,
        out_specs=P(("grp", "rhs", "sub"), "br", None),
        check_vma=False,
    )
```
